512 devices in a mesh: dp: 32 (over x, y), tensor: 16 (over z, core).
Axes of the slice: x: 4, y: 8, z: 8, core: 2. Of those that a mesh axis runs over, the one named last changes fastest.
Arguments:
- normed: bfloat16 [32768, 1536], P('dp', 'tensor'), may hold values from -6 to 6
- cotangent: bfloat16 [32768, 6144], P('dp', 'tensor'), may hold values from -6 to 6
- weight: bfloat16 [1536, 6144], P(None, 'tensor'), may hold values from -0.15625 to 0.15625
- error: bfloat16 [32, 1536, 6144], P('dp', None, 'tensor'), may hold values from -48 to 48
- q_init: float32 [32, 6144], P(None, 'tensor'), may hold values from -6 to 6
- lengths: int32 [128], P('dp'), may hold values from 64 to 256
- film_scale: float32 [128, 1536], P('dp'), may hold values from 0.1 to 1.9
- film_shift: float32 [128, 1536], P('dp'), may hold values from -3 to 3
Outputs:
- d_normed: bfloat16 [32768, 1536], P('dp', 'tensor')
- d_scale: float32 [128, 1536], P('dp', 'tensor')
- d_shift: float32 [128, 1536], P('dp', 'tensor')
- p_factor: float32 [16, 32, 1536], P('tensor')
- q_next: float32 [32, 6144], P(None, 'tensor')
- new_error: bfloat16 [32, 1536, 6144], P('dp', None, 'tensor')
The draws below stay inside these ranges and needn't reach their ends.
All inputs are finite; a program needn't handle non-finite values.
Results may differ from the reference program's by a relative error of at most 0.023.
Values may be sent and summed in bfloat16 or wider, within the bound.
No kernel may reach another device: no remote copies, remote signals or barrier semaphores. Data moves between devices by JAX's collectives and lax.ppermute only.
A program may use at most 64 MiB of HBM per device.

```python
import jax
import jax.numpy as jnp
from jax import lax

D = 1536
FFW = 6144
RANK = 32
SEQ = 256
TOK_DEV = 1024
SAMP_DEV = 4
SAMPLES = 128
TOKENS = 32768
N_DP = 32
N_TENSOR = 16


def plant(drawn, stream_key, smallest, high):
    spot = [jax.random.randint(jax.random.fold_in(stream_key, axis), (), 0, length) for axis, length in enumerate(drawn.shape)]
    main_axis = drawn.shape.index(max(drawn.shape))
    beside = spot[:main_axis] + [(spot[main_axis] + 1) % drawn.shape[main_axis]] + spot[main_axis + 1:]
    return drawn.at[tuple(spot)].set(smallest).at[tuple(beside)].set(high)


def levels(rng, dims, shards, low, largest):
    level, own = 1.0, jax.random.fold_in(rng, 6)
    for dim, shards_of in shards:
        steps = jnp.exp(jax.random.uniform(jax.random.fold_in(own, dim), (shards_of,), jnp.float32, low / len(shards), largest / len(shards)))
        level = level * jnp.repeat(steps, dims[dim] // shards_of).reshape([-1 if axis == dim else 1 for axis in range(len(dims))])
    return level


def bell_draw(own_key, shape, scale, limit, cuts=(), kind=jnp.bfloat16):
    values = scale * jax.random.normal(own_key, shape, jnp.float32)
    if cuts:
        values = values * levels(own_key, shape, cuts, -0.22, 0.18)
    return jnp.clip(values, -limit, limit).astype(kind)


def setup_inputs(seed: int = 0) -> dict:
    keys = jax.random.split(jax.random.key(seed), 9)
    normed = bell_draw(keys[0], (TOKENS, D), 1.0, 6.0, ((0, 32), (1, 16)))
    cotangent = bell_draw(keys[1], (TOKENS, FFW), 1.0, 6.0, ((0, 32), (1, 16)))
    weight = bell_draw(keys[2], (D, FFW), D ** -0.5, 0.15625, ((1, 16),))
    error = bell_draw(keys[3], (N_DP, D, FFW), 8.0, 48.0, ((0, 32), (2, 16)))
    q_init = bell_draw(keys[4], (RANK, FFW), 1.0, 6.0, ((1, 16),), jnp.float32)
    lengths = plant(jax.random.randint(keys[5], (SAMPLES,), SEQ // 4, SEQ + 1), jax.random.fold_in(keys[5], 1), SEQ // 4, SEQ).astype(jnp.int32)
    film_scale = jnp.clip(1.0 + 0.18 * jax.random.normal(keys[6], (SAMPLES, D), jnp.float32), 0.1, 1.9)
    film_shift = bell_draw(keys[7], (SAMPLES, D), 0.5, 3.0, ((0, 32),), jnp.float32)
    return {"normed": normed, "cotangent": cotangent, "weight": weight, "error": error, "q_init": q_init, "lengths": lengths, "film_scale": film_scale, "film_shift": film_shift}


def gelu_slope(u):
    cdf = 0.5 * (1.0 + lax.erf(u * 0.7071067811865476))
    dens = jnp.exp(-0.5 * u * u) * 0.3989422804014327
    return cdf + u * dens

def orthonormal(pmat):

    def one_column(j, basis):
        column = lax.dynamic_slice_in_dim(pmat, j, 1, 1)
        coeffs = jnp.dot(basis.T, column, precision=lax.Precision.HIGHEST)
        column = column - jnp.dot(basis, coeffs, precision=lax.Precision.HIGHEST)
        column = column / (jnp.sqrt(jnp.sum(column * column)) + 1e-06)
        return lax.dynamic_update_slice_in_dim(basis, column, j, 1)
    return lax.fori_loop(0, pmat.shape[1], one_column, jnp.zeros_like(pmat))

def reference(normed, cotangent, weight, error, q_init, lengths, film_scale, film_shift):
    groups = N_TENSOR
    group_width = FFW // groups
    position = jnp.arange(TOK_DEV, dtype=jnp.int32)
    sample_local = position // SEQ
    within = position % SEQ
    onehot = (sample_local[:, None] == jnp.arange(SAMP_DEV, dtype=jnp.int32)[None, :]).astype(jnp.float32)
    weight_groups = weight.reshape(D, groups, group_width).astype(jnp.float32)

    def replica(inputs):
        index, error_r = inputs
        rows = lax.dynamic_slice_in_dim(normed, index * TOK_DEV, TOK_DEV, 0)
        cot = lax.dynamic_slice_in_dim(cotangent, index * TOK_DEV, TOK_DEV, 0)
        samples = index * SAMP_DEV + sample_local
        scale_rows = film_scale[samples]
        shift_rows = film_shift[samples]
        valid = (within < lengths[samples]).astype(jnp.float32)
        z_rows = (rows.astype(jnp.float32) * scale_rows + shift_rows).astype(jnp.bfloat16)
        u = jnp.dot(z_rows, weight, preferred_element_type=jnp.float32)
        d_pre = (cot.astype(jnp.float32) * gelu_slope(u) * valid[:, None]).astype(jnp.bfloat16)
        moment = jnp.dot(z_rows.T, d_pre, preferred_element_type=jnp.float32) + error_r.astype(jnp.float32)
        parts = jnp.einsum('tgf,dgf->gtd', d_pre.reshape(TOK_DEV, groups, group_width).astype(jnp.float32), weight_groups)
        parts = lax.optimization_barrier(parts.astype(jnp.bfloat16))
        dz = lax.optimization_barrier(jnp.sum(parts.astype(jnp.float32), axis=0))
        d_normed = (dz * scale_rows).astype(jnp.bfloat16)
        d_scale = jnp.dot(onehot.T, dz * rows.astype(jnp.float32), precision=lax.Precision.HIGHEST)
        d_shift = jnp.dot(onehot.T, dz, precision=lax.Precision.HIGHEST)
        return (d_normed, d_scale, d_shift, moment)
    d_normed, d_scale, d_shift, moment = lax.map(replica, (jnp.arange(N_DP, dtype=jnp.int32), error))
    moment = moment.reshape(N_DP, D, groups, group_width)
    q_groups = q_init.reshape(RANK, groups, group_width)
    p_raw = jnp.einsum('rdgf,kgf->gdk', moment, q_groups, precision=lax.Precision.HIGHEST)
    p_hat = jax.vmap(orthonormal)(p_raw)
    q_new = jnp.einsum('rdgf,gdk->gkf', moment, p_hat, precision=lax.Precision.HIGHEST) / N_DP
    averaged = jnp.einsum('gdk,gkf->dgf', p_hat, q_new, precision=lax.Precision.HIGHEST)
    new_error = (moment - averaged[None]).astype(jnp.bfloat16).reshape(N_DP, D, FFW)
    p_factor = jnp.transpose(p_hat, (0, 2, 1))
    q_next = jnp.transpose(q_new, (1, 0, 2)).reshape(RANK, FFW)
    return (d_normed.reshape(TOKENS, D), d_scale.reshape(SAMPLES, D), d_shift.reshape(SAMPLES, D), p_factor, q_next, new_error)
```

```python
import functools

import jax
import jax.numpy as jnp
from jax import lax
from jax.experimental import pallas as pl
from jax.experimental.pallas import tpu as pltpu
from jax.sharding import Mesh, PartitionSpec as P

SEQ = 256
DP = ("x", "y")
TENSOR = ("z", "core")
BF = jnp.bfloat16
F32 = jnp.float32
NN = (((1,), (0,)), ((), ()))
NT = (((1,), (1,)), ((), ()))
TN = (((0,), (0,)), ((), ()))
MIB = 1024 * 1024


def mm(a, b, dims):
    return lax.dot_general(a, b, dims, preferred_element_type=F32)


def split(v):
    hi = v.astype(BF)
    return hi, (v - hi.astype(F32)).astype(BF)


def gelu_slope(u):
    cdf = 0.5 * (1.0 + lax.erf(u * 0.7071067811865476))
    dens = jnp.exp(-0.5 * u * u) * 0.3989422804014327
    return cdf + u * dens


def backward_kernel(lengths, rows, w_t, weight, cot_t, film, error, q_init,
                    part, moment, p_out, film_t, z_buf):
    s = pl.program_id(0)
    samples = pl.num_programs(0)

    @pl.when(s == 0)
    def _():
        film_t[...] = film[...].T

    for k in range(4):
        @pl.when(s == k)
        def _(k=k):
            scale = film_t[:, k:k + 1]
            shift = film_t[:, 4 + k:5 + k]
            z_buf[...] = (rows[...].astype(F32) * scale + shift).astype(BF)

    z = z_buf[...]
    u = mm(w_t[...], z, NN)
    position = lax.broadcasted_iota(jnp.int32, (1, SEQ), 1)
    valid = (position < lengths[s]).astype(F32)
    d_pre = (cot_t[...].astype(F32) * gelu_slope(u) * valid).astype(BF)
    part[...] = mm(weight[...], d_pre, NN).astype(BF)
    product = mm(z, d_pre, NT)

    @pl.when(s == 0)
    def _():
        moment[...] = product + error[0].astype(F32)

    @pl.when(s > 0)
    def _():
        moment[...] += product

    @pl.when(s == samples - 1)
    def _():
        m_hi, m_lo = split(moment[...])
        q_hi, q_lo = split(q_init[...])
        rank = q_init.shape[0]
        first = mm(jnp.concatenate([q_hi, q_lo], axis=0), m_hi, NT)
        p = first[:rank] + first[rank:] + mm(q_hi, m_lo, NT)
        for k in range(rank):
            p_out[k] = p[k:k + 1]


def backward(lengths, rows, w_t, weight, cot_t, film, error, q_init):
    width, tokens = rows.shape
    hidden = weight.shape[1]
    rank = q_init.shape[0]
    whole = lambda *shape: pl.BlockSpec(shape, lambda s: (0,) * len(shape))
    return pl.pallas_call(
        backward_kernel,
        grid=(tokens // SEQ,),
        in_specs=[
            pl.BlockSpec(memory_space=pltpu.SMEM),
            pl.BlockSpec((width, SEQ), lambda s: (0, s)),
            whole(hidden, width),
            whole(width, hidden),
            pl.BlockSpec((hidden, SEQ), lambda s: (0, s)),
            whole(8, width),
            whole(1, width, hidden),
            whole(rank, hidden),
        ],
        out_specs=[
            pl.BlockSpec((width, SEQ), lambda s: (0, s)),
            whole(width, hidden),
            whole(rank, 1, width),
        ],
        out_shape=[
            jax.ShapeDtypeStruct((width, tokens), BF),
            jax.ShapeDtypeStruct((width, hidden), F32),
            jax.ShapeDtypeStruct((rank, 1, width), F32),
        ],
        scratch_shapes=[pltpu.VMEM((width, 8), F32), pltpu.VMEM((width, SEQ), BF)],
        compiler_params=pltpu.CompilerParams(vmem_limit_bytes=48 * MIB),
        cost_estimate=pl.CostEstimate(
            flops=6 * tokens * width * hidden, bytes_accessed=14 * MIB, transcendentals=0
        ),
    )(lengths, rows, w_t, weight, cot_t, film, error, q_init)


def right_kernel(p_rows, moment, y_out):
    rank = p_rows.shape[0]
    p = jnp.concatenate([p_rows[k] for k in range(rank)], axis=0)
    p_hi, p_lo = split(p)
    m_hi, m_lo = split(moment[...])
    first = mm(jnp.concatenate([p_hi, p_lo], axis=0), m_hi, NN)
    y_out[...] = (first[:rank] + first[rank:] + mm(p_hi, m_lo, NN)).astype(BF)


def right_factor(p_rows, moment):
    rank = p_rows.shape[0]
    width, hidden = moment.shape
    return pl.pallas_call(
        right_kernel,
        out_shape=jax.ShapeDtypeStruct((rank, hidden), BF),
        compiler_params=pltpu.CompilerParams(vmem_limit_bytes=32 * MIB),
        cost_estimate=pl.CostEstimate(
            flops=6 * rank * width * hidden, bytes_accessed=3 * MIB, transcendentals=0
        ),
    )(p_rows, moment)


def gram_schmidt_kernel(p_rows, basis_out, mix_out, p, work):
    rank, _, width = p_rows.shape
    for k in range(rank):
        p[pl.ds(k, 1), :] = p_rows[k]
        work[pl.ds(k, 1), :width] = p_rows[k]
    row_id = lax.broadcasted_iota(jnp.int32, (rank, 1), 0)
    eye_row = lax.broadcasted_iota(jnp.int32, (rank, 128), 0)
    eye_col = lax.broadcasted_iota(jnp.int32, (rank, 128), 1)
    work[:, width:] = (eye_row == eye_col).astype(F32)

    def step(i, carry):
        row = work[pl.ds(i, 1), :]
        main = row[:, :width]
        norm = jnp.sqrt(jnp.sum(main * main, axis=1, keepdims=True))
        unit = row / (norm + 1e-06)
        coeffs = jnp.sum(p[...] * unit[:, :width], axis=1, keepdims=True)
        coeffs = jnp.where(row_id > i, coeffs, 0.0)
        work[...] = jnp.where(row_id == i, unit, work[...] - coeffs * unit)
        return carry

    lax.fori_loop(0, rank, step, 0)
    basis_out[...] = work[:, :width]
    mix_out[...] = work[:, width:]


def gram_schmidt(p_rows):
    rank, _, width = p_rows.shape
    return pl.pallas_call(
        gram_schmidt_kernel,
        out_shape=[
            jax.ShapeDtypeStruct((rank, width), F32),
            jax.ShapeDtypeStruct((rank, 128), F32),
        ],
        scratch_shapes=[pltpu.VMEM((rank, width), F32), pltpu.VMEM((rank, width + 128), F32)],
        compiler_params=pltpu.CompilerParams(vmem_limit_bytes=16 * MIB),
        cost_estimate=pl.CostEstimate(
            flops=4 * rank * rank * width, bytes_accessed=MIB, transcendentals=0
        ),
    )(p_rows)


def finish_kernel(replicas, y_parts, mix, basis, moment, q_out, error_out, q_buf):
    rank = q_out.shape[0]

    @pl.when(pl.program_id(0) == 0)
    def _():
        y = y_parts[0].astype(F32)
        for k in range(1, y_parts.shape[0]):
            y = y + y_parts[k].astype(F32)
        y_hi, y_lo = split(y * (1.0 / replicas))
        a_hi, a_lo = split(mix[:, :rank])
        q_new = mm(a_hi, y_hi, NN) + mm(a_lo, y_hi, NN) + mm(a_hi, y_lo, NN)
        q_out[...] = q_new
        q_hi, q_lo = split(q_new)
        q_buf[...] = jnp.concatenate([q_hi, q_hi, q_lo], axis=0)

    b_hi, b_lo = split(basis[...])
    averaged = mm(jnp.concatenate([b_hi, b_lo, b_hi], axis=0), q_buf[...], TN)
    error_out[0] = (moment[...] - averaged).astype(BF)


def finish(replicas, y_parts, mix, basis, moment):
    width, hidden = moment.shape
    rank = basis.shape[0]
    block = width // 4
    return pl.pallas_call(
        functools.partial(finish_kernel, replicas),
        grid=(4,),
        in_specs=[
            pl.BlockSpec(y_parts.shape, lambda i: (0, 0, 0)),
            pl.BlockSpec(mix.shape, lambda i: (0, 0)),
            pl.BlockSpec((rank, block), lambda i: (0, i)),
            pl.BlockSpec((block, hidden), lambda i: (i, 0)),
        ],
        out_specs=[
            pl.BlockSpec((rank, hidden), lambda i: (0, 0)),
            pl.BlockSpec((1, block, hidden), lambda i: (0, i, 0)),
        ],
        out_shape=[
            jax.ShapeDtypeStruct((rank, hidden), F32),
            jax.ShapeDtypeStruct((1, width, hidden), BF),
        ],
        scratch_shapes=[pltpu.VMEM((3 * rank, hidden), BF)],
        compiler_params=pltpu.CompilerParams(vmem_limit_bytes=16 * MIB),
        cost_estimate=pl.CostEstimate(
            flops=6 * rank * width * hidden, bytes_accessed=4 * MIB, transcendentals=0
        ),
    )(y_parts, mix, basis, moment)


def film_kernel(dz_t, rows, scale_t, d_normed, d_scale, d_shift):
    width, tokens = dz_t.shape
    samples = scale_t.shape[1]
    dz = dz_t[...]
    wide = dz.astype(F32)
    for k in range(samples):
        cut = slice(k * SEQ, (k + 1) * SEQ)
        d_normed[:, cut] = (wide[:, cut] * scale_t[:, k:k + 1]).astype(BF)
    sample = lax.broadcasted_iota(jnp.int32, (8, tokens), 0)
    token = lax.broadcasted_iota(jnp.int32, (8, tokens), 1)
    table = (token // SEQ == sample).astype(BF)
    hi, lo = split(wide * rows[...].astype(F32))
    d_scale[...] = (mm(table, hi, NT) + mm(table, lo, NT))[:samples]
    d_shift[...] = mm(table, dz, NT)[:samples]


def film_gradients(dz_t, rows, scale_t):
    width, tokens = dz_t.shape
    samples = scale_t.shape[1]
    return pl.pallas_call(
        film_kernel,
        out_shape=[
            jax.ShapeDtypeStruct((width, tokens), BF),
            jax.ShapeDtypeStruct((samples, width), F32),
            jax.ShapeDtypeStruct((samples, width), F32),
        ],
        compiler_params=pltpu.CompilerParams(vmem_limit_bytes=16 * MIB),
        cost_estimate=pl.CostEstimate(
            flops=64 * tokens * width, bytes_accessed=MIB, transcendentals=0
        ),
    )(dz_t, rows, scale_t)


def local(normed, cotangent, weight, error, q_init, lengths, film_scale, film_shift):
    replicas = lax.axis_size(DP)
    col_width = normed.shape[1]
    rank, hidden = q_init.shape
    own = normed.T
    rows = lax.all_gather(own, TENSOR, axis=0, tiled=True)
    film = jnp.concatenate([film_scale, film_shift], axis=0)
    part, moment, p_local = backward(
        lengths, rows, weight.T, weight, cotangent.T, film, error, q_init
    )

    dz = lax.psum_scatter(part, TENSOR, scatter_dimension=0, tiled=True)
    start = lax.axis_index(TENSOR) * col_width
    own_scale = lax.dynamic_slice_in_dim(film_scale, start, col_width, 1).T
    d_normed, d_scale, d_shift = film_gradients(dz, own, own_scale)

    p_parts = lax.all_to_all(p_local, DP, 0, 0, tiled=True)
    p_row = jnp.sum(p_parts, axis=0)
    p_rows = lax.all_to_all(
        jnp.broadcast_to(p_row[None], (replicas,) + p_row.shape), DP, 0, 0, tiled=True
    )
    y = right_factor(p_rows, moment)
    basis, mix = gram_schmidt(p_rows)
    nx, ny = lax.axis_size("x"), lax.axis_size("y")
    y_x = lax.all_to_all(jnp.broadcast_to(y[None], (nx, rank, hidden)), "x", 0, 0, tiled=True)
    y = jnp.sum(y_x.astype(F32), axis=0).astype(BF)
    y_y = lax.all_to_all(jnp.broadcast_to(y[None], (ny, rank, hidden)), "y", 0, 0, tiled=True)
    q_new, new_error = finish(replicas, y_y, mix, basis, moment)
    return (d_normed.T, d_scale, d_shift, basis[None], q_new, new_error)


def solution(mesh):
    x, y, z = 4, 8, 8
    grid = Mesh(mesh.devices.reshape(x, y, z, 2), ("x", "y", "z", "core"))
    return jax.shard_map(
        local,
        mesh=grid,
        in_specs=(
            P(DP, TENSOR),
            P(DP, TENSOR),
            P(None, TENSOR),
            P(DP, None, TENSOR),
            P(None, TENSOR),
            P(DP),
            P(DP, None),
            P(DP, None),
        ),
        out_specs=(
            P(DP, TENSOR),
            P(DP, TENSOR),
            P(DP, TENSOR),
            P(TENSOR, None, None),
            P(None, TENSOR),
            P(DP, None, TENSOR),
        ),
        check_vma=False,
    )
```

```python
import functools

import jax
import jax.numpy as jnp
from jax import lax
from jax.experimental import pallas as pl
from jax.experimental.pallas import tpu as pltpu
from jax.sharding import Mesh, PartitionSpec as P

SEQ = 256
DP = ("x", "y")
TENSOR = ("z", "core")
SWAP = [(0, 1), (1, 0)]
BF = jnp.bfloat16
F32 = jnp.float32
NN = (((1,), (0,)), ((), ()))
NT = (((1,), (1,)), ((), ()))
TN = (((0,), (0,)), ((), ()))
MIB = 1024 * 1024
CHUNKS = 3
IN_VMEM = pl.BlockSpec(memory_space=pltpu.VMEM)
IN_HBM = pl.BlockSpec(memory_space=pltpu.HBM)


def mm(a, b, dims):
    return lax.dot_general(a, b, dims, preferred_element_type=F32)


def split(v):
    hi = v.astype(BF)
    return hi, (v - hi.astype(F32)).astype(BF)


def gelu_slope(u):
    cdf = 0.5 * (1.0 + lax.erf(u * 0.7071067811865476))
    dens = jnp.exp(-0.5 * u * u) * 0.3989422804014327
    return cdf + u * dens


def backward_kernel(lengths, rows, w_t, weight, cot_t, film, error, q_init,
                    part, moment, p_out,
                    row_buf, wt_buf, w_buf, cot_buf, err_buf, z_buf, part_buf, m_buf, sems):
    width = rows.shape[0]
    rank = q_init.shape[0]
    samples = lengths.shape[0]
    step = width // CHUNKS
    cuts = [pl.ds(c * step, step) for c in range(CHUNKS)]
    sem = iter(range(sems.shape[0]))

    def fetch(source, target):
        copy = pltpu.make_async_copy(source, target, sems.at[next(sem)])
        copy.start()
        return copy

    get_rows = [fetch(rows.at[cuts[0]], row_buf.at[cuts[0]])]
    get_wt = fetch(w_t, wt_buf)
    get_rows += [fetch(rows.at[cut], row_buf.at[cut]) for cut in cuts[1:]]
    get_cot = fetch(cot_t, cot_buf)
    get_w = fetch(weight, w_buf)
    get_error = fetch(error.at[0], err_buf)

    film_t = film[...].T
    u = None
    for c in range(CHUNKS):
        cut = slice(c * step, (c + 1) * step)
        get_rows[c].wait()
        z = jnp.concatenate(
            [
                (
                    row_buf[cut, k * SEQ:(k + 1) * SEQ].astype(F32) * film_t[cut, k:k + 1]
                    + film_t[cut, samples + k:samples + k + 1]
                ).astype(BF)
                for k in range(samples)
            ],
            axis=1,
        )
        z_buf[cut, :] = z
        if c == 0:
            get_wt.wait()
        term = mm(wt_buf[:, cut], z, NN)
        u = term if u is None else u + term
    position = lax.broadcasted_iota(jnp.int32, (1, SEQ), 1)
    valid = jnp.concatenate(
        [(position < lengths[k]).astype(F32) for k in range(samples)], axis=1
    )
    get_cot.wait()
    d_pre = (cot_buf[...].astype(F32) * gelu_slope(u) * valid).astype(BF)
    get_w.wait()
    puts = []
    for c in range(CHUNKS):
        cut = slice(c * step, (c + 1) * step)
        part_buf[cut, :] = mm(w_buf[cut, :], d_pre, NN).astype(BF)
        puts.append(fetch(part_buf.at[cuts[c]], part.at[cuts[c]]))
    get_error.wait()
    q_hi, q_lo = split(q_init[...])
    q_both = jnp.concatenate([q_hi, q_lo], axis=0)
    for c in range(CHUNKS):
        cut = slice(c * step, (c + 1) * step)
        total = mm(z_buf[cut, :], d_pre, NT) + err_buf[cut, :].astype(F32)
        m_buf[cut, :] = total
        puts.append(fetch(m_buf.at[cuts[c]], moment.at[cuts[c]]))
        m_hi, m_lo = split(total)
        first = mm(q_both, m_hi, NT)
        p = first[:rank] + first[rank:] + mm(q_hi, m_lo, NT)
        for k in range(rank):
            p_out[k, :, cut] = p[k:k + 1]
    for put in puts:
        put.wait()


def backward(lengths, rows, w_t, weight, cot_t, film, error, q_init):
    width, tokens = rows.shape
    rank, hidden = q_init.shape
    return pl.pallas_call(
        backward_kernel,
        in_specs=[pl.BlockSpec(memory_space=pltpu.SMEM)]
        + [IN_HBM] * 4 + [IN_VMEM, IN_HBM, IN_VMEM],
        out_specs=[IN_HBM, IN_HBM, IN_VMEM],
        out_shape=[
            jax.ShapeDtypeStruct((width, tokens), BF),
            jax.ShapeDtypeStruct((width, hidden), F32),
            jax.ShapeDtypeStruct((rank, 1, width), F32),
        ],
        scratch_shapes=[
            pltpu.VMEM((width, tokens), BF),
            pltpu.VMEM((hidden, width), BF),
            pltpu.VMEM((width, hidden), BF),
            pltpu.VMEM((hidden, tokens), BF),
            pltpu.VMEM((width, hidden), BF),
            pltpu.VMEM((width, tokens), BF),
            pltpu.VMEM((width, tokens), BF),
            pltpu.VMEM((width, hidden), F32),
            pltpu.SemaphoreType.DMA((3 * CHUNKS + 4,)),
        ],
        compiler_params=pltpu.CompilerParams(vmem_limit_bytes=58 * MIB),
        cost_estimate=pl.CostEstimate(
            flops=6 * tokens * width * hidden, bytes_accessed=14 * MIB, transcendentals=0
        ),
    )(lengths, rows, w_t, weight, cot_t, film, error, q_init)


def right_kernel(p_rows, moment, y_out):
    rank = p_rows.shape[0]
    p = jnp.concatenate([p_rows[k] for k in range(rank)], axis=0)
    p_hi, p_lo = split(p)
    m_hi, m_lo = split(moment[...])
    first = mm(jnp.concatenate([p_hi, p_lo], axis=0), m_hi, NN)
    y_out[...] = (first[:rank] + first[rank:] + mm(p_hi, m_lo, NN)).astype(BF)


def right_factor(p_rows, moment):
    rank = p_rows.shape[0]
    width, hidden = moment.shape
    return pl.pallas_call(
        right_kernel,
        out_shape=jax.ShapeDtypeStruct((rank, hidden), BF),
        compiler_params=pltpu.CompilerParams(vmem_limit_bytes=32 * MIB),
        cost_estimate=pl.CostEstimate(
            flops=6 * rank * width * hidden, bytes_accessed=3 * MIB, transcendentals=0
        ),
    )(p_rows, moment)


def gram_schmidt_kernel(p_rows, basis_out, mix_out, stack_out, p, work):
    rank, _, width = p_rows.shape
    for k in range(rank):
        p[k:k + 1, :] = p_rows[k]
        work[k:k + 1, :width] = p_rows[k]
    eye_row = lax.broadcasted_iota(jnp.int32, (rank, 128), 0)
    eye_col = lax.broadcasted_iota(jnp.int32, (rank, 128), 1)
    work[:, width:] = (eye_row == eye_col).astype(F32)
    for i in range(rank):
        top = i // 8 * 8
        row_id = lax.broadcasted_iota(jnp.int32, (rank - top, 1), 0) + top
        row = work[i:i + 1, :]
        main = row[:, :width]
        square = jnp.sum(main * main, axis=1, keepdims=True)
        dots = jnp.sum(p[top:, :] * main, axis=1, keepdims=True)
        inverse = 1.0 / (jnp.sqrt(square) + 1e-06)
        unit = row * inverse
        coeffs = jnp.where(row_id > i, dots * inverse, 0.0)
        work[top:, :] = jnp.where(row_id == i, unit, work[top:, :] - coeffs * unit)
    basis = work[:, :width]
    basis_out[...] = basis
    mix_out[...] = work[:, width:]
    hi, lo = split(basis)
    stack_out[...] = jnp.concatenate([hi, lo, hi], axis=0)


def gram_schmidt(p_rows):
    rank, _, width = p_rows.shape
    return pl.pallas_call(
        gram_schmidt_kernel,
        out_shape=[
            jax.ShapeDtypeStruct((rank, width), F32),
            jax.ShapeDtypeStruct((rank, 128), F32),
            jax.ShapeDtypeStruct((3 * rank, width), BF),
        ],
        scratch_shapes=[pltpu.VMEM((rank, width), F32), pltpu.VMEM((rank, width + 128), F32)],
        compiler_params=pltpu.CompilerParams(vmem_limit_bytes=16 * MIB),
        cost_estimate=pl.CostEstimate(
            flops=4 * rank * rank * width, bytes_accessed=MIB, transcendentals=0
        ),
    )(p_rows)


def finish_kernel(replicas, y_parts, mix, stack, moment, q_out, error_out, q_buf):
    rank = q_out.shape[0]

    @pl.when(pl.program_id(0) == 0)
    def _():
        y = y_parts[0].astype(F32)
        for k in range(1, y_parts.shape[0]):
            y = y + y_parts[k].astype(F32)
        y_hi, y_lo = split(y * (1.0 / replicas))
        a_hi, a_lo = split(mix[:, :rank])
        q_new = mm(a_hi, y_hi, NN) + mm(a_lo, y_hi, NN) + mm(a_hi, y_lo, NN)
        q_out[...] = q_new
        q_hi, q_lo = split(q_new)
        q_buf[...] = jnp.concatenate([q_hi, q_hi, q_lo], axis=0)

    averaged = mm(stack[...], q_buf[...], TN)
    error_out[0] = (moment[...] - averaged).astype(BF)


def finish(replicas, y_parts, mix, stack, moment):
    width, hidden = moment.shape
    rank = mix.shape[0]
    block = width // 4
    return pl.pallas_call(
        functools.partial(finish_kernel, replicas),
        grid=(4,),
        in_specs=[
            pl.BlockSpec(y_parts.shape, lambda i: (0, 0, 0)),
            pl.BlockSpec(mix.shape, lambda i: (0, 0)),
            pl.BlockSpec((3 * rank, block), lambda i: (0, i)),
            pl.BlockSpec((block, hidden), lambda i: (i, 0)),
        ],
        out_specs=[
            pl.BlockSpec((rank, hidden), lambda i: (0, 0)),
            pl.BlockSpec((1, block, hidden), lambda i: (0, i, 0)),
        ],
        out_shape=[
            jax.ShapeDtypeStruct((rank, hidden), F32),
            jax.ShapeDtypeStruct((1, width, hidden), BF),
        ],
        scratch_shapes=[pltpu.VMEM((3 * rank, hidden), BF)],
        compiler_params=pltpu.CompilerParams(vmem_limit_bytes=16 * MIB),
        cost_estimate=pl.CostEstimate(
            flops=6 * rank * width * hidden, bytes_accessed=4 * MIB, transcendentals=0
        ),
    )(y_parts, mix, stack, moment)


def film_kernel(core, dz_own, dz_peer, rows, scale_t, d_normed, d_scale, d_shift):
    _, width, tokens = dz_own.shape
    samples = scale_t.shape[1]
    wide = dz_own[core[0]].astype(F32) + dz_peer[core[0]].astype(F32)
    for k in range(samples):
        cut = slice(k * SEQ, (k + 1) * SEQ)
        d_normed[:, cut] = (wide[:, cut] * scale_t[:, k:k + 1]).astype(BF)
    sample = lax.broadcasted_iota(jnp.int32, (8, tokens), 0)
    token = lax.broadcasted_iota(jnp.int32, (8, tokens), 1)
    table = (token // SEQ == sample).astype(BF)
    hi, lo = split(wide * rows[...].astype(F32))
    d_scale[...] = (mm(table, hi, NT) + mm(table, lo, NT))[:samples]
    hi, lo = split(wide)
    d_shift[...] = (mm(table, hi, NT) + mm(table, lo, NT))[:samples]


def film_gradients(core, dz_own, dz_peer, rows, scale_t):
    _, width, tokens = dz_own.shape
    samples = scale_t.shape[1]
    return pl.pallas_call(
        film_kernel,
        in_specs=[pl.BlockSpec(memory_space=pltpu.SMEM)] + [IN_VMEM] * 4,
        out_shape=[
            jax.ShapeDtypeStruct((width, tokens), BF),
            jax.ShapeDtypeStruct((samples, width), F32),
            jax.ShapeDtypeStruct((samples, width), F32),
        ],
        compiler_params=pltpu.CompilerParams(vmem_limit_bytes=16 * MIB),
        cost_estimate=pl.CostEstimate(
            flops=64 * tokens * width, bytes_accessed=MIB, transcendentals=0
        ),
    )(core, dz_own, dz_peer, rows, scale_t)


def local(normed, cotangent, weight, error, q_init, lengths, film_scale, film_shift):
    replicas = lax.axis_size(DP)
    col_width = normed.shape[1]
    rank, hidden = q_init.shape
    own = normed.T
    rows = lax.all_gather(own, TENSOR, axis=0, tiled=True)
    film = jnp.concatenate([film_scale, film_shift], axis=0)
    core = lax.axis_index("core")
    start = lax.axis_index(TENSOR) * col_width
    own_scale = lax.dynamic_slice_in_dim(film_scale, start, col_width, 1).T
    film, own_scale = lax.optimization_barrier((film, own_scale))
    part, moment, p_local = backward(
        lengths, rows, weight.T, weight, cotangent.T, film, error, q_init
    )

    dz_pair = lax.psum_scatter(part, "z", scatter_dimension=0, tiled=True)
    dz_pair = dz_pair.reshape(2, col_width, -1)
    dz_peer = lax.ppermute(dz_pair, "core", SWAP)
    d_normed, d_scale, d_shift = film_gradients(
        core.reshape(1), dz_pair, dz_peer, own, own_scale
    )

    p_parts = lax.all_to_all(p_local, DP, 0, 0, tiled=True)
    p_row = jnp.sum(p_parts, axis=0)
    p_rows = lax.all_to_all(
        jnp.broadcast_to(p_row[None], (replicas,) + p_row.shape), DP, 0, 0, tiled=True
    )
    y = right_factor(p_rows, moment)
    basis, mix, stack = gram_schmidt(p_rows)
    nx, ny = lax.axis_size("x"), lax.axis_size("y")
    y_x = lax.all_to_all(jnp.broadcast_to(y[None], (nx, rank, hidden)), "x", 0, 0, tiled=True)
    y = jnp.sum(y_x.astype(F32), axis=0).astype(BF)
    y_y = lax.all_to_all(jnp.broadcast_to(y[None], (ny, rank, hidden)), "y", 0, 0, tiled=True)
    q_new, new_error = finish(replicas, y_y, mix, stack, moment)
    return (d_normed.T, d_scale, d_shift, basis[None], q_new, new_error)


def solution(mesh):
    x, y, z = 4, 8, 8
    grid = Mesh(mesh.devices.reshape(x, y, z, 2), ("x", "y", "z", "core"))
    return jax.shard_map(
        local,
        mesh=grid,
        in_specs=(
            P(DP, TENSOR),
            P(DP, TENSOR),
            P(None, TENSOR),
            P(DP, None, TENSOR),
            P(None, TENSOR),
            P(DP),
            P(DP, None),
            P(DP, None),
        ),
        out_specs=(
            P(DP, TENSOR),
            P(DP, TENSOR),
            P(DP, TENSOR),
            P(TENSOR, None, None),
            P(None, TENSOR),
            P(DP, None, TENSOR),
        ),
        check_vma=False,
    )
```

```python
import functools

import jax
import jax.numpy as jnp
from jax import lax
from jax.experimental import pallas as pl
from jax.experimental.pallas import tpu as pltpu
from jax.sharding import Mesh, PartitionSpec as P

SEQ = 256
DP = ("x", "y")
TENSOR = ("z", "core")
SWAP = [(0, 1), (1, 0)]
BF = jnp.bfloat16
F32 = jnp.float32
NN = (((1,), (0,)), ((), ()))
NT = (((1,), (1,)), ((), ()))
TN = (((0,), (0,)), ((), ()))
MIB = 1024 * 1024
CHUNKS = 3
IN_VMEM = pl.BlockSpec(memory_space=pltpu.VMEM)
IN_HBM = pl.BlockSpec(memory_space=pltpu.HBM)


def mm(a, b, dims):
    return lax.dot_general(a, b, dims, preferred_element_type=F32)


def split(v):
    hi = v.astype(BF)
    return hi, (v - hi.astype(F32)).astype(BF)


def gelu_slope(u):
    cdf = 0.5 * (1.0 + lax.erf(u * 0.7071067811865476))
    dens = jnp.exp(-0.5 * u * u) * 0.3989422804014327
    return cdf + u * dens


def backward_kernel(lengths, rows, w_t, weight, cot_t, film, error, q_init,
                    part, moment, p_out,
                    row_buf, wt_buf, w_buf, cot_buf, err_buf, z_buf, part_buf, m_buf, sems):
    width = rows.shape[0]
    rank = q_init.shape[0]
    samples = lengths.shape[0]
    step = width // CHUNKS
    cuts = [pl.ds(c * step, step) for c in range(CHUNKS)]
    sem = iter(range(sems.shape[0]))

    def fetch(source, target):
        copy = pltpu.make_async_copy(source, target, sems.at[next(sem)])
        copy.start()
        return copy

    get_rows = [fetch(rows.at[cuts[0]], row_buf.at[cuts[0]])]
    get_wt = fetch(w_t, wt_buf)
    get_rows += [fetch(rows.at[cut], row_buf.at[cut]) for cut in cuts[1:]]
    get_cot = fetch(cot_t, cot_buf)
    get_w = fetch(weight, w_buf)
    get_error = fetch(error.at[0], err_buf)

    film_t = film[...].T
    u = None
    for c in range(CHUNKS):
        cut = slice(c * step, (c + 1) * step)
        get_rows[c].wait()
        z = jnp.concatenate(
            [
                (
                    row_buf[cut, k * SEQ:(k + 1) * SEQ].astype(F32) * film_t[cut, k:k + 1]
                    + film_t[cut, samples + k:samples + k + 1]
                ).astype(BF)
                for k in range(samples)
            ],
            axis=1,
        )
        z_buf[cut, :] = z
        if c == 0:
            get_wt.wait()
        term = mm(wt_buf[:, cut], z, NN)
        u = term if u is None else u + term
    position = lax.broadcasted_iota(jnp.int32, (1, SEQ), 1)
    valid = jnp.concatenate(
        [(position < lengths[k]).astype(F32) for k in range(samples)], axis=1
    )
    get_cot.wait()
    d_pre = (cot_buf[...].astype(F32) * gelu_slope(u) * valid).astype(BF)
    get_w.wait()
    puts = []
    for c in range(CHUNKS):
        cut = slice(c * step, (c + 1) * step)
        part_buf[cut, :] = mm(w_buf[cut, :], d_pre, NN).astype(BF)
        puts.append(fetch(part_buf.at[cuts[c]], part.at[cuts[c]]))
    get_error.wait()
    q_hi, q_lo = split(q_init[...])
    q_both = jnp.concatenate([q_hi, q_lo], axis=0)
    for c in range(CHUNKS):
        cut = slice(c * step, (c + 1) * step)
        total = mm(z_buf[cut, :], d_pre, NT) + err_buf[cut, :].astype(F32)
        m_buf[cut, :] = total
        puts.append(fetch(m_buf.at[cuts[c]], moment.at[cuts[c]]))
        m_hi, m_lo = split(total)
        first = mm(q_both, m_hi, NT)
        p = first[:rank] + first[rank:] + mm(q_hi, m_lo, NT)
        for k in range(rank):
            p_out[k, :, cut] = p[k:k + 1]
    for put in puts:
        put.wait()


def backward(lengths, rows, w_t, weight, cot_t, film, error, q_init):
    width, tokens = rows.shape
    rank, hidden = q_init.shape
    return pl.pallas_call(
        backward_kernel,
        in_specs=[pl.BlockSpec(memory_space=pltpu.SMEM)]
        + [IN_HBM] * 4 + [IN_VMEM, IN_HBM, IN_VMEM],
        out_specs=[IN_HBM, IN_HBM, IN_VMEM],
        out_shape=[
            jax.ShapeDtypeStruct((width, tokens), BF),
            jax.ShapeDtypeStruct((width, hidden), F32),
            jax.ShapeDtypeStruct((rank, 1, width), F32),
        ],
        scratch_shapes=[
            pltpu.VMEM((width, tokens), BF),
            pltpu.VMEM((hidden, width), BF),
            pltpu.VMEM((width, hidden), BF),
            pltpu.VMEM((hidden, tokens), BF),
            pltpu.VMEM((width, hidden), BF),
            pltpu.VMEM((width, tokens), BF),
            pltpu.VMEM((width, tokens), BF),
            pltpu.VMEM((width, hidden), F32),
            pltpu.SemaphoreType.DMA((3 * CHUNKS + 4,)),
        ],
        compiler_params=pltpu.CompilerParams(vmem_limit_bytes=50 * MIB),
        cost_estimate=pl.CostEstimate(
            flops=6 * tokens * width * hidden, bytes_accessed=14 * MIB, transcendentals=0
        ),
    )(lengths, rows, w_t, weight, cot_t, film, error, q_init)


def right_kernel(p_rows, moment, y_out):
    rank = p_rows.shape[0]
    p = jnp.concatenate([p_rows[k] for k in range(rank)], axis=0)
    p_hi, p_lo = split(p)
    m_hi, m_lo = split(moment[...])
    first = mm(jnp.concatenate([p_hi, p_lo], axis=0), m_hi, NN)
    y_out[...] = (first[:rank] + first[rank:] + mm(p_hi, m_lo, NN)).astype(BF)


def right_factor(p_rows, moment):
    rank = p_rows.shape[0]
    width, hidden = moment.shape
    return pl.pallas_call(
        right_kernel,
        out_shape=jax.ShapeDtypeStruct((rank, hidden), BF),
        compiler_params=pltpu.CompilerParams(vmem_limit_bytes=32 * MIB),
        cost_estimate=pl.CostEstimate(
            flops=600_000_000, bytes_accessed=MIB, transcendentals=0
        ),
    )(p_rows, moment)


def gram_schmidt_kernel(p_rows, basis_out, mix_out, stack_out, p, work):
    rank, _, width = p_rows.shape
    for k in range(rank):
        p[k:k + 1, :] = p_rows[k]
        work[k:k + 1, :width] = p_rows[k]
    eye_row = lax.broadcasted_iota(jnp.int32, (rank, 128), 0)
    eye_col = lax.broadcasted_iota(jnp.int32, (rank, 128), 1)
    work[:, width:] = (eye_row == eye_col).astype(F32)
    for i in range(rank):
        top = i // 8 * 8
        row_id = lax.broadcasted_iota(jnp.int32, (rank - top, 1), 0) + top
        row = work[i:i + 1, :]
        main = row[:, :width]
        square = jnp.sum(main * main, axis=1, keepdims=True)
        dots = jnp.sum(p[top:, :] * main, axis=1, keepdims=True)
        inverse = 1.0 / (jnp.sqrt(square) + 1e-06)
        unit = row * inverse
        coeffs = jnp.where(row_id > i, dots * inverse, 0.0)
        work[top:, :] = jnp.where(row_id == i, unit, work[top:, :] - coeffs * unit)
    basis = work[:, :width]
    basis_out[...] = basis
    mix_out[...] = work[:, width:]
    hi, lo = split(basis)
    stack_out[...] = jnp.concatenate([hi, lo, hi], axis=0)


def gram_schmidt(p_rows):
    rank, _, width = p_rows.shape
    return pl.pallas_call(
        gram_schmidt_kernel,
        out_shape=[
            jax.ShapeDtypeStruct((rank, width), F32),
            jax.ShapeDtypeStruct((rank, 128), F32),
            jax.ShapeDtypeStruct((3 * rank, width), BF),
        ],
        scratch_shapes=[pltpu.VMEM((rank, width), F32), pltpu.VMEM((rank, width + 128), F32)],
        compiler_params=pltpu.CompilerParams(vmem_limit_bytes=16 * MIB),
        cost_estimate=pl.CostEstimate(
            flops=5_300_000_000, bytes_accessed=MIB, transcendentals=0
        ),
    )(p_rows)


def finish_kernel(replicas, y_parts, mix, stack, moment, q_out, error_out, q_buf):
    rank = q_out.shape[0]

    @pl.when(pl.program_id(0) == 0)
    def _():
        y = y_parts[0].astype(F32)
        for k in range(1, y_parts.shape[0]):
            y = y + y_parts[k].astype(F32)
        y_hi, y_lo = split(y * (1.0 / replicas))
        a_hi, a_lo = split(mix[:, :rank])
        q_new = mm(a_hi, y_hi, NN) + mm(a_lo, y_hi, NN) + mm(a_hi, y_lo, NN)
        q_out[...] = q_new
        q_hi, q_lo = split(q_new)
        q_buf[...] = jnp.concatenate([q_hi, q_hi, q_lo], axis=0)

    averaged = mm(stack[...], q_buf[...], TN)
    error_out[0] = (moment[...] - averaged).astype(BF)


def finish(replicas, y_parts, mix, stack, moment):
    width, hidden = moment.shape
    rank = mix.shape[0]
    block = width // 4
    return pl.pallas_call(
        functools.partial(finish_kernel, replicas),
        grid=(4,),
        in_specs=[
            pl.BlockSpec(y_parts.shape, lambda i: (0, 0, 0)),
            pl.BlockSpec(mix.shape, lambda i: (0, 0)),
            pl.BlockSpec((3 * rank, block), lambda i: (0, i)),
            pl.BlockSpec((block, hidden), lambda i: (i, 0)),
        ],
        out_specs=[
            pl.BlockSpec((rank, hidden), lambda i: (0, 0)),
            pl.BlockSpec((1, block, hidden), lambda i: (0, i, 0)),
        ],
        out_shape=[
            jax.ShapeDtypeStruct((rank, hidden), F32),
            jax.ShapeDtypeStruct((1, width, hidden), BF),
        ],
        scratch_shapes=[pltpu.VMEM((3 * rank, hidden), BF)],
        compiler_params=pltpu.CompilerParams(vmem_limit_bytes=16 * MIB),
        cost_estimate=pl.CostEstimate(
            flops=2_900_000_000, bytes_accessed=4 * MIB, transcendentals=0
        ),
    )(y_parts, mix, stack, moment)


def film_kernel(core, dz_own, dz_peer, rows, scale_t, d_normed, d_scale, d_shift):
    _, width, tokens = dz_own.shape
    samples = scale_t.shape[1]
    wide = dz_own[core[0]].astype(F32) + dz_peer[core[0]].astype(F32)
    for k in range(samples):
        cut = slice(k * SEQ, (k + 1) * SEQ)
        d_normed[:, cut] = (wide[:, cut] * scale_t[:, k:k + 1]).astype(BF)
    sample = lax.broadcasted_iota(jnp.int32, (8, tokens), 0)
    token = lax.broadcasted_iota(jnp.int32, (8, tokens), 1)
    table = (token // SEQ == sample).astype(BF)
    hi, lo = split(wide * rows[...].astype(F32))
    d_scale[...] = (mm(table, hi, NT) + mm(table, lo, NT))[:samples]
    hi, lo = split(wide)
    d_shift[...] = (mm(table, hi, NT) + mm(table, lo, NT))[:samples]


def film_gradients(core, dz_own, dz_peer, rows, scale_t):
    _, width, tokens = dz_own.shape
    samples = scale_t.shape[1]
    return pl.pallas_call(
        film_kernel,
        in_specs=[pl.BlockSpec(memory_space=pltpu.SMEM)] + [IN_VMEM] * 4,
        out_shape=[
            jax.ShapeDtypeStruct((width, tokens), BF),
            jax.ShapeDtypeStruct((samples, width), F32),
            jax.ShapeDtypeStruct((samples, width), F32),
        ],
        compiler_params=pltpu.CompilerParams(vmem_limit_bytes=16 * MIB),
        cost_estimate=pl.CostEstimate(
            flops=1_100_000_000, bytes_accessed=MIB, transcendentals=0
        ),
    )(core, dz_own, dz_peer, rows, scale_t)


def local(normed, cotangent, weight, error, q_init, lengths, film_scale, film_shift):
    replicas = lax.axis_size(DP)
    col_width = normed.shape[1]
    rank, hidden = q_init.shape
    own = normed.T
    rows = lax.all_gather(own, TENSOR, axis=0, tiled=True)
    film = jnp.concatenate([film_scale, film_shift], axis=0)
    core = lax.axis_index("core")
    start = lax.axis_index(TENSOR) * col_width
    own_scale = lax.dynamic_slice_in_dim(film_scale, start, col_width, 1).T
    film, own_scale = lax.optimization_barrier((film, own_scale))
    part, moment, p_local = backward(
        lengths, rows, weight.T, weight, cotangent.T, film, error, q_init
    )

    dz_pair = lax.psum_scatter(part, "z", scatter_dimension=0, tiled=True)
    dz_pair = dz_pair.reshape(2, col_width, -1)
    p_parts = lax.all_to_all(p_local, DP, 0, 0, tiled=True)
    p_row = jnp.sum(p_parts, axis=0)
    p_rows = lax.all_to_all(
        jnp.broadcast_to(p_row[None], (replicas,) + p_row.shape), DP, 0, 0, tiled=True
    )
    y = right_factor(p_rows, moment)
    nx, ny = lax.axis_size("x"), lax.axis_size("y")
    y_x = lax.all_to_all(jnp.broadcast_to(y[None], (nx, rank, hidden)), "x", 0, 0, tiled=True)
    y = jnp.sum(y_x.astype(F32), axis=0).astype(BF)
    p_late, _ = lax.optimization_barrier((p_rows, y))
    basis, mix, stack = gram_schmidt(p_late)
    dz_pair, _ = lax.optimization_barrier((dz_pair, mix))
    dz_peer = lax.ppermute(dz_pair, "core", SWAP)
    d_normed, d_scale, d_shift = film_gradients(
        core.reshape(1), dz_pair, dz_peer, own, own_scale
    )
    y_y = lax.all_to_all(jnp.broadcast_to(y[None], (ny, rank, hidden)), "y", 0, 0, tiled=True)
    q_new, new_error = finish(replicas, y_y, mix, stack, moment)
    return (d_normed.T, d_scale, d_shift, basis[None], q_new, new_error)


def solution(mesh):
    x, y, z = 4, 8, 8
    grid = Mesh(mesh.devices.reshape(x, y, z, 2), ("x", "y", "z", "core"))
    return jax.shard_map(
        local,
        mesh=grid,
        in_specs=(
            P(DP, TENSOR),
            P(DP, TENSOR),
            P(None, TENSOR),
            P(DP, None, TENSOR),
            P(None, TENSOR),
            P(DP),
            P(DP, None),
            P(DP, None),
        ),
        out_specs=(
            P(DP, TENSOR),
            P(DP, TENSOR),
            P(DP, TENSOR),
            P(TENSOR, None, None),
            P(None, TENSOR),
            P(DP, None, TENSOR),
        ),
        check_vma=False,
    )
```

```python
import functools

import jax
import jax.numpy as jnp
from jax import lax
from jax.experimental import pallas as pl
from jax.experimental.pallas import tpu as pltpu
from jax.sharding import Mesh, PartitionSpec as P

SEQ = 256
DP = ("x", "y")
TENSOR = ("z", "core")
SWAP = [(0, 1), (1, 0)]
BF = jnp.bfloat16
F32 = jnp.float32
NN = (((1,), (0,)), ((), ()))
NT = (((1,), (1,)), ((), ()))
TN = (((0,), (0,)), ((), ()))
MIB = 1024 * 1024
CHUNKS = 3
HALVES = 2
IN_VMEM = pl.BlockSpec(memory_space=pltpu.VMEM)
IN_HBM = pl.BlockSpec(memory_space=pltpu.HBM)


def mm(a, b, dims):
    return lax.dot_general(a, b, dims, preferred_element_type=F32)


def split(v):
    hi = v.astype(BF)
    return hi, (v - hi.astype(F32)).astype(BF)


def gelu_slope(u):
    cdf = 0.5 * (1.0 + lax.erf(u * 0.7071067811865476))
    dens = jnp.exp(-0.5 * u * u) * 0.3989422804014327
    return cdf + u * dens


def backward_kernel(lengths, rows, w_t, weight, cot_t, film, error, q_init,
                    part, moment, p_out,
                    row_buf, wt_buf, w_buf, cot_buf, err_buf, z_buf, part_buf, m_buf, sems):
    width = rows.shape[0]
    rank = q_init.shape[0]
    samples = lengths.shape[0]
    step = width // CHUNKS
    cuts = [pl.ds(c * step, step) for c in range(CHUNKS)]
    sem = iter(range(sems.shape[0]))

    def fetch(source, target):
        copy = pltpu.make_async_copy(source, target, sems.at[next(sem)])
        copy.start()
        return copy

    get_rows = [fetch(rows.at[cuts[0]], row_buf.at[cuts[0]])]
    get_wt = fetch(w_t, wt_buf)
    get_rows += [fetch(rows.at[cut], row_buf.at[cut]) for cut in cuts[1:]]
    get_cot = fetch(cot_t, cot_buf)
    get_w = fetch(weight, w_buf)
    get_error = fetch(error.at[0], err_buf)

    film_t = film[...].T
    for c in range(CHUNKS):
        cut = slice(c * step, (c + 1) * step)
        get_rows[c].wait()
        for k in range(samples):
            z_buf[cut, k * SEQ:(k + 1) * SEQ] = (
                row_buf[cut, k * SEQ:(k + 1) * SEQ].astype(F32) * film_t[cut, k:k + 1]
                + film_t[cut, samples + k:samples + k + 1]
            ).astype(BF)
    get_wt.wait()
    get_cot.wait()
    position = lax.broadcasted_iota(jnp.int32, (1, SEQ), 1)
    halves = []
    for h in range(HALVES):
        span = samples // HALVES
        cols = slice(h * span * SEQ, (h + 1) * span * SEQ)
        u = mm(wt_buf[...], z_buf[:, cols], NN)
        valid = jnp.concatenate(
            [(position < lengths[k]).astype(F32) for k in range(h * span, (h + 1) * span)], axis=1
        )
        halves.append((cot_buf[:, cols].astype(F32) * gelu_slope(u) * valid).astype(BF))
    d_pre = jnp.concatenate(halves, axis=1)
    get_w.wait()
    puts = []
    for c in range(CHUNKS):
        cut = slice(c * step, (c + 1) * step)
        part_buf[cut, :] = mm(w_buf[cut, :], d_pre, NN).astype(BF)
        puts.append(fetch(part_buf.at[cuts[c]], part.at[cuts[c]]))
    get_error.wait()
    q_hi, q_lo = split(q_init[...])
    q_both = jnp.concatenate([q_hi, q_lo], axis=0)
    p_parts = []
    for c in range(CHUNKS):
        cut = slice(c * step, (c + 1) * step)
        total = mm(z_buf[cut, :], d_pre, NT) + err_buf[cut, :].astype(F32)
        m_buf[cut, :] = total
        puts.append(fetch(m_buf.at[cuts[c]], moment.at[cuts[c]]))
        m_hi, m_lo = split(total)
        first = mm(q_both, m_hi, NT)
        p = first[:rank] + first[rank:] + mm(q_hi, m_lo, NT)
        p_parts.append(p)
    p = jnp.concatenate(p_parts, axis=1)
    half = width // 2
    for k in range(rank):
        p_out[k] = jnp.concatenate([p[k:k + 1, :half], p[k:k + 1, half:]], axis=0).astype(BF)
    for put in puts:
        put.wait()


def backward(lengths, rows, w_t, weight, cot_t, film, error, q_init):
    width, tokens = rows.shape
    rank, hidden = q_init.shape
    return pl.pallas_call(
        backward_kernel,
        in_specs=[pl.BlockSpec(memory_space=pltpu.SMEM)]
        + [IN_HBM] * 4 + [IN_VMEM, IN_HBM, IN_VMEM],
        out_specs=[IN_HBM, IN_HBM, IN_VMEM],
        out_shape=[
            jax.ShapeDtypeStruct((width, tokens), BF),
            jax.ShapeDtypeStruct((width, hidden), F32),
            jax.ShapeDtypeStruct((rank, 2, width // 2), BF),
        ],
        scratch_shapes=[
            pltpu.VMEM((width, tokens), BF),
            pltpu.VMEM((hidden, width), BF),
            pltpu.VMEM((width, hidden), BF),
            pltpu.VMEM((hidden, tokens), BF),
            pltpu.VMEM((width, hidden), BF),
            pltpu.VMEM((width, tokens), BF),
            pltpu.VMEM((width, tokens), BF),
            pltpu.VMEM((width, hidden), F32),
            pltpu.SemaphoreType.DMA((3 * CHUNKS + 4,)),
        ],
        compiler_params=pltpu.CompilerParams(vmem_limit_bytes=50 * MIB),
        cost_estimate=pl.CostEstimate(
            flops=6 * tokens * width * hidden, bytes_accessed=14 * MIB, transcendentals=0
        ),
    )(lengths, rows, w_t, weight, cot_t, film, error, q_init)


def right_kernel(p_rows, moment, y_out):
    rank = p_rows.shape[0]
    rows = [p_rows[k].astype(F32) for k in range(rank)]
    p = jnp.concatenate(
        [jnp.concatenate([row[h:h + 1] for row in rows], axis=0) for h in range(2)], axis=1
    ).astype(BF)
    m_hi, m_lo = split(moment[...])
    y_out[...] = (mm(p, m_hi, NN) + mm(p, m_lo, NN)).astype(BF)


def right_factor(p_rows, moment):
    rank = p_rows.shape[0]
    width, hidden = moment.shape
    return pl.pallas_call(
        right_kernel,
        out_shape=jax.ShapeDtypeStruct((rank, hidden), BF),
        compiler_params=pltpu.CompilerParams(vmem_limit_bytes=32 * MIB),
        cost_estimate=pl.CostEstimate(
            flops=600_000_000, bytes_accessed=MIB, transcendentals=0
        ),
    )(p_rows, moment)


def gram_schmidt_kernel(p_rows, basis_out, mix_out, stack_out, p, work):
    rank, _, half = p_rows.shape
    width = 2 * half
    for k in range(rank):
        row = p_rows[k].astype(F32)
        row = jnp.concatenate([row[:1], row[1:]], axis=1)
        p[k:k + 1, :] = row
        work[k:k + 1, :width] = row
    eye_row = lax.broadcasted_iota(jnp.int32, (rank, 128), 0)
    eye_col = lax.broadcasted_iota(jnp.int32, (rank, 128), 1)
    work[:, width:] = (eye_row == eye_col).astype(F32)
    for i in range(rank):
        top = i // 8 * 8
        row_id = lax.broadcasted_iota(jnp.int32, (rank - top, 1), 0) + top
        row = work[i:i + 1, :]
        main = row[:, :width]
        square = jnp.sum(main * main, axis=1, keepdims=True)
        dots = jnp.sum(p[top:, :] * main, axis=1, keepdims=True)
        inverse = 1.0 / (jnp.sqrt(square) + 1e-06)
        unit = row * inverse
        coeffs = jnp.where(row_id > i, dots * inverse, 0.0)
        work[top:, :] = jnp.where(row_id == i, unit, work[top:, :] - coeffs * unit)
    basis = work[:, :width]
    basis_out[...] = basis
    mix_out[...] = work[:, width:]
    hi, lo = split(basis)
    stack_out[...] = jnp.concatenate([hi, lo, hi], axis=0)


def gram_schmidt(p_rows):
    rank, _, half = p_rows.shape
    width = 2 * half
    return pl.pallas_call(
        gram_schmidt_kernel,
        out_shape=[
            jax.ShapeDtypeStruct((rank, width), F32),
            jax.ShapeDtypeStruct((rank, 128), F32),
            jax.ShapeDtypeStruct((3 * rank, width), BF),
        ],
        scratch_shapes=[pltpu.VMEM((rank, width), F32), pltpu.VMEM((rank, width + 128), F32)],
        compiler_params=pltpu.CompilerParams(vmem_limit_bytes=16 * MIB),
        cost_estimate=pl.CostEstimate(
            flops=5_300_000_000, bytes_accessed=MIB, transcendentals=0
        ),
    )(p_rows)


def finish_kernel(replicas, y_parts, mix, stack, moment, q_out, error_out, buf, sems):
    rank = q_out.shape[0]
    y = y_parts[0].astype(F32)
    for k in range(1, y_parts.shape[0]):
        y = y + y_parts[k].astype(F32)
    y_hi, y_lo = split(y * (1.0 / replicas))
    a_hi, a_lo = split(mix[:, :rank])
    q_new = mm(a_hi, y_hi, NN) + mm(a_lo, y_hi, NN) + mm(a_hi, y_lo, NN)
    q_out[...] = q_new
    q_hi, q_lo = split(q_new)
    q_stack = jnp.concatenate([q_hi, q_hi, q_lo], axis=0)
    step = moment.shape[0] // CHUNKS
    puts = []
    for c in range(CHUNKS):
        cut = slice(c * step, (c + 1) * step)
        averaged = mm(stack[:, cut], q_stack, TN)
        buf[cut, :] = (moment[cut, :] - averaged).astype(BF)
        put = pltpu.make_async_copy(
            buf.at[pl.ds(c * step, step)], error_out.at[0, pl.ds(c * step, step)], sems.at[c]
        )
        put.start()
        puts.append(put)
    for put in puts:
        put.wait()


def finish(replicas, y_parts, mix, stack, moment):
    width, hidden = moment.shape
    rank = mix.shape[0]
    return pl.pallas_call(
        functools.partial(finish_kernel, replicas),
        out_specs=[IN_VMEM, IN_HBM],
        out_shape=[
            jax.ShapeDtypeStruct((rank, hidden), F32),
            jax.ShapeDtypeStruct((1, width, hidden), BF),
        ],
        scratch_shapes=[
            pltpu.VMEM((width, hidden), BF),
            pltpu.SemaphoreType.DMA((CHUNKS,)),
        ],
        compiler_params=pltpu.CompilerParams(vmem_limit_bytes=16 * MIB),
        cost_estimate=pl.CostEstimate(
            flops=2_500_000_000, bytes_accessed=4 * MIB, transcendentals=0
        ),
    )(y_parts, mix, stack, moment)


def film_kernel(core, dz_own, dz_peer, rows, scale_t, d_normed, d_scale, d_shift):
    _, width, tokens = dz_own.shape
    samples = scale_t.shape[1]
    wide = dz_own[core[0]].astype(F32) + dz_peer[core[0]].astype(F32)
    for k in range(samples):
        cut = slice(k * SEQ, (k + 1) * SEQ)
        d_normed[:, cut] = (wide[:, cut] * scale_t[:, k:k + 1]).astype(BF)
    sample = lax.broadcasted_iota(jnp.int32, (8, tokens), 0)
    token = lax.broadcasted_iota(jnp.int32, (8, tokens), 1)
    table = (token // SEQ == sample).astype(BF)
    hi, lo = split(wide * rows[...].astype(F32))
    d_scale[...] = (mm(table, hi, NT) + mm(table, lo, NT))[:samples]
    hi, lo = split(wide)
    d_shift[...] = (mm(table, hi, NT) + mm(table, lo, NT))[:samples]


def film_gradients(core, dz_own, dz_peer, rows, scale_t):
    _, width, tokens = dz_own.shape
    samples = scale_t.shape[1]
    return pl.pallas_call(
        film_kernel,
        in_specs=[pl.BlockSpec(memory_space=pltpu.SMEM)] + [IN_VMEM] * 4,
        out_shape=[
            jax.ShapeDtypeStruct((width, tokens), BF),
            jax.ShapeDtypeStruct((samples, width), F32),
            jax.ShapeDtypeStruct((samples, width), F32),
        ],
        compiler_params=pltpu.CompilerParams(vmem_limit_bytes=16 * MIB),
        cost_estimate=pl.CostEstimate(
            flops=1_100_000_000, bytes_accessed=MIB, transcendentals=0
        ),
    )(core, dz_own, dz_peer, rows, scale_t)


def local(normed, cotangent, weight, error, q_init, lengths, film_scale, film_shift):
    replicas = lax.axis_size(DP)
    col_width = normed.shape[1]
    rank, hidden = q_init.shape
    own = normed.T
    rows = lax.all_gather(own, TENSOR, axis=0, tiled=True)
    film = jnp.concatenate([film_scale, film_shift], axis=0)
    core = lax.axis_index("core")
    start = lax.axis_index(TENSOR) * col_width
    own_scale = lax.dynamic_slice_in_dim(film_scale, start, col_width, 1).T
    film, own_scale = lax.optimization_barrier((film, own_scale))
    part, moment, p_local = backward(
        lengths, rows, weight.T, weight, cotangent.T, film, error, q_init
    )

    dz_pair = lax.psum_scatter(part, "z", scatter_dimension=0, tiled=True)
    dz_pair = dz_pair.reshape(2, col_width, -1)
    p_parts = lax.all_to_all(p_local, DP, 0, 0, tiled=True)
    p_row = jnp.sum(p_parts.astype(F32), axis=0).astype(BF)
    p_rows = lax.all_to_all(
        jnp.broadcast_to(p_row[None], (replicas,) + p_row.shape), DP, 0, 0, tiled=True
    )
    y = right_factor(p_rows, moment)
    nx, ny = lax.axis_size("x"), lax.axis_size("y")
    y_x = lax.all_to_all(jnp.broadcast_to(y[None], (nx, rank, hidden)), "x", 0, 0, tiled=True)
    y = jnp.sum(y_x.astype(F32), axis=0).astype(BF)
    p_late, _ = lax.optimization_barrier((p_rows, y))
    basis, mix, stack = gram_schmidt(p_late)
    dz_pair, _ = lax.optimization_barrier((dz_pair, mix))
    dz_peer = lax.ppermute(dz_pair, "core", SWAP)
    d_normed, d_scale, d_shift = film_gradients(
        core.reshape(1), dz_pair, dz_peer, own, own_scale
    )
    y_y = lax.all_to_all(jnp.broadcast_to(y[None], (ny, rank, hidden)), "y", 0, 0, tiled=True)
    q_new, new_error = finish(replicas, y_y, mix, stack, moment)
    return (d_normed.T, d_scale, d_shift, basis[None], q_new, new_error)


def solution(mesh):
    x, y, z = 4, 8, 8
    grid = Mesh(mesh.devices.reshape(x, y, z, 2), ("x", "y", "z", "core"))
    return jax.shard_map(
        local,
        mesh=grid,
        in_specs=(
            P(DP, TENSOR),
            P(DP, TENSOR),
            P(None, TENSOR),
            P(DP, None, TENSOR),
            P(None, TENSOR),
            P(DP),
            P(DP, None),
            P(DP, None),
        ),
        out_specs=(
            P(DP, TENSOR),
            P(DP, TENSOR),
            P(DP, TENSOR),
            P(TENSOR, None, None),
            P(None, TENSOR),
            P(DP, None, TENSOR),
        ),
        check_vma=False,
    )
```

```python
import functools

import jax
import jax.numpy as jnp
from jax import lax
from jax.experimental import pallas as pl
from jax.experimental.pallas import tpu as pltpu
from jax.sharding import Mesh, PartitionSpec as P

SEQ = 256
DP = ("x", "y")
TENSOR = ("z", "core")
SWAP = [(0, 1), (1, 0)]
BF = jnp.bfloat16
F32 = jnp.float32
NN = (((1,), (0,)), ((), ()))
NT = (((1,), (1,)), ((), ()))
TN = (((0,), (0,)), ((), ()))
MIB = 1024 * 1024
CHUNKS = 3
HALVES = 2
IN_VMEM = pl.BlockSpec(memory_space=pltpu.VMEM)
IN_HBM = pl.BlockSpec(memory_space=pltpu.HBM)


def mm(a, b, dims):
    return lax.dot_general(a, b, dims, preferred_element_type=F32)


def split(v):
    hi = v.astype(BF)
    return hi, (v - hi.astype(F32)).astype(BF)


def gelu_slope(u):
    cdf = 0.5 * (1.0 + lax.erf(u * 0.7071067811865476))
    dens = jnp.exp(-0.5 * u * u) * 0.3989422804014327
    return cdf + u * dens


def backward_kernel(lengths, rows, w_t, weight, cot_t, film, p_error, q_init,
                    part, z_out, d_out, p_out,
                    row_buf, wt_buf, w_buf, cot_buf, z_buf, part_buf, sems):
    width = rows.shape[0]
    rank = q_init.shape[0]
    samples = lengths.shape[0]
    step = width // CHUNKS
    cuts = [pl.ds(c * step, step) for c in range(CHUNKS)]
    sem = iter(range(sems.shape[0]))

    def fetch(source, target):
        copy = pltpu.make_async_copy(source, target, sems.at[next(sem)])
        copy.start()
        return copy

    get_rows = [fetch(rows.at[cuts[0]], row_buf.at[cuts[0]])]
    get_wt = fetch(w_t, wt_buf)
    get_rows += [fetch(rows.at[cut], row_buf.at[cut]) for cut in cuts[1:]]
    get_cot = fetch(cot_t, cot_buf)
    get_w = fetch(weight, w_buf)

    film_t = film[...].T
    puts = []
    for c in range(CHUNKS):
        cut = slice(c * step, (c + 1) * step)
        get_rows[c].wait()
        for k in range(samples):
            z_buf[cut, k * SEQ:(k + 1) * SEQ] = (
                row_buf[cut, k * SEQ:(k + 1) * SEQ].astype(F32) * film_t[cut, k:k + 1]
                + film_t[cut, samples + k:samples + k + 1]
            ).astype(BF)
        puts.append(fetch(z_buf.at[cuts[c]], z_out.at[cuts[c]]))
    get_wt.wait()
    get_cot.wait()
    position = lax.broadcasted_iota(jnp.int32, (1, SEQ), 1)
    halves = []
    for h in range(HALVES):
        span = samples // HALVES
        cols = slice(h * span * SEQ, (h + 1) * span * SEQ)
        u = mm(wt_buf[...], z_buf[:, cols], NN)
        valid = jnp.concatenate(
            [(position < lengths[k]).astype(F32) for k in range(h * span, (h + 1) * span)], axis=1
        )
        halves.append((cot_buf[:, cols].astype(F32) * gelu_slope(u) * valid).astype(BF))
    d_pre = jnp.concatenate(halves, axis=1)
    d_out[...] = d_pre
    get_w.wait()
    for c in range(CHUNKS):
        cut = slice(c * step, (c + 1) * step)
        part_buf[cut, :] = mm(w_buf[cut, :], d_pre, NN).astype(BF)
        puts.append(fetch(part_buf.at[cuts[c]], part.at[cuts[c]]))
    q_hi, q_lo = split(q_init[...])
    qd = mm(jnp.concatenate([q_hi, q_lo], axis=0), d_pre, NN)
    s_hi, s_lo = split(qd[:rank] + qd[rank:])
    both = mm(jnp.concatenate([s_hi, s_lo], axis=0), z_buf[...], NT)
    p = both[:rank] + both[rank:] + p_error[...]
    half = width // 2
    for k in range(rank):
        p_out[k] = jnp.concatenate([p[k:k + 1, :half], p[k:k + 1, half:]], axis=0).astype(BF)
    for put in puts:
        put.wait()


def backward(lengths, rows, w_t, weight, cot_t, film, p_error, q_init):
    width, tokens = rows.shape
    rank, hidden = q_init.shape
    return pl.pallas_call(
        backward_kernel,
        in_specs=[pl.BlockSpec(memory_space=pltpu.SMEM)]
        + [IN_HBM] * 4 + [IN_VMEM] * 3,
        out_specs=[IN_HBM, IN_HBM, IN_VMEM, IN_VMEM],
        out_shape=[
            jax.ShapeDtypeStruct((width, tokens), BF),
            jax.ShapeDtypeStruct((width, tokens), BF),
            jax.ShapeDtypeStruct((hidden, tokens), BF),
            jax.ShapeDtypeStruct((rank, 2, width // 2), BF),
        ],
        scratch_shapes=[
            pltpu.VMEM((width, tokens), BF),
            pltpu.VMEM((hidden, width), BF),
            pltpu.VMEM((width, hidden), BF),
            pltpu.VMEM((hidden, tokens), BF),
            pltpu.VMEM((width, tokens), BF),
            pltpu.VMEM((width, tokens), BF),
            pltpu.SemaphoreType.DMA((3 * CHUNKS + 3,)),
        ],
        compiler_params=pltpu.CompilerParams(vmem_limit_bytes=50 * MIB),
        cost_estimate=pl.CostEstimate(
            flops=10_000_000_000, bytes_accessed=14 * MIB, transcendentals=0
        ),
    )(lengths, rows, w_t, weight, cot_t, film, p_error, q_init)


def error_kernel(error, q_init, out):
    rank = q_init.shape[0]
    q_hi, q_lo = split(q_init[...])
    both = mm(jnp.concatenate([q_hi, q_lo], axis=0), error[0], NT)
    out[...] = both[:rank] + both[rank:]


def error_share(error, q_init):
    rank, hidden = q_init.shape
    width = error.shape[1]
    return pl.pallas_call(
        error_kernel,
        out_shape=jax.ShapeDtypeStruct((rank, width), F32),
        compiler_params=pltpu.CompilerParams(vmem_limit_bytes=16 * MIB),
        cost_estimate=pl.CostEstimate(
            flops=1_000_000_000, bytes_accessed=2 * MIB, transcendentals=0
        ),
    )(error, q_init)


def moment_kernel(z, d_pre, error, out):
    out[...] = mm(z[...], d_pre[...], NT) + error[0].astype(F32)


def moment_of(z, d_pre, error):
    width, tokens = z.shape
    hidden = d_pre.shape[0]
    step = width // CHUNKS
    return pl.pallas_call(
        moment_kernel,
        grid=(CHUNKS,),
        in_specs=[
            pl.BlockSpec((step, tokens), lambda i: (i, 0)),
            IN_VMEM,
            pl.BlockSpec((1, step, hidden), lambda i: (0, i, 0)),
        ],
        out_specs=pl.BlockSpec((step, hidden), lambda i: (i, 0)),
        out_shape=jax.ShapeDtypeStruct((width, hidden), F32),
        compiler_params=pltpu.CompilerParams(vmem_limit_bytes=20 * MIB),
        cost_estimate=pl.CostEstimate(
            flops=3_500_000_000, bytes_accessed=6 * MIB, transcendentals=0
        ),
    )(z, d_pre, error)


def right_kernel(p_rows, moment, y_out):
    rank = p_rows.shape[0]
    rows = [p_rows[k].astype(F32) for k in range(rank)]
    p = jnp.concatenate(
        [jnp.concatenate([row[h:h + 1] for row in rows], axis=0) for h in range(2)], axis=1
    ).astype(BF)
    m_hi, m_lo = split(moment[...])
    y_out[...] = (mm(p, m_hi, NN) + mm(p, m_lo, NN)).astype(BF)


def right_factor(p_rows, moment):
    rank = p_rows.shape[0]
    width, hidden = moment.shape
    return pl.pallas_call(
        right_kernel,
        out_shape=jax.ShapeDtypeStruct((rank, hidden), BF),
        compiler_params=pltpu.CompilerParams(vmem_limit_bytes=32 * MIB),
        cost_estimate=pl.CostEstimate(
            flops=600_000_000, bytes_accessed=MIB, transcendentals=0
        ),
    )(p_rows, moment)


def gram_schmidt_kernel(p_rows, basis_out, mix_out, stack_out, p, work):
    rank, _, half = p_rows.shape
    width = 2 * half
    for k in range(rank):
        row = p_rows[k].astype(F32)
        row = jnp.concatenate([row[:1], row[1:]], axis=1)
        p[k:k + 1, :] = row
        work[k:k + 1, :width] = row
    eye_row = lax.broadcasted_iota(jnp.int32, (rank, 128), 0)
    eye_col = lax.broadcasted_iota(jnp.int32, (rank, 128), 1)
    work[:, width:] = (eye_row == eye_col).astype(F32)
    for i in range(rank):
        top = i // 8 * 8
        row_id = lax.broadcasted_iota(jnp.int32, (rank - top, 1), 0) + top
        row = work[i:i + 1, :]
        main = row[:, :width]
        square = jnp.sum(main * main, axis=1, keepdims=True)
        dots = jnp.sum(p[top:, :] * main, axis=1, keepdims=True)
        inverse = 1.0 / (jnp.sqrt(square) + 1e-06)
        unit = row * inverse
        coeffs = jnp.where(row_id > i, dots * inverse, 0.0)
        work[top:, :] = jnp.where(row_id == i, unit, work[top:, :] - coeffs * unit)
    basis = work[:, :width]
    basis_out[...] = basis
    mix_out[...] = work[:, width:]
    hi, lo = split(basis)
    stack_out[...] = jnp.concatenate([hi, lo, hi], axis=0)


def gram_schmidt(p_rows):
    rank, _, half = p_rows.shape
    width = 2 * half
    return pl.pallas_call(
        gram_schmidt_kernel,
        out_shape=[
            jax.ShapeDtypeStruct((rank, width), F32),
            jax.ShapeDtypeStruct((rank, 128), F32),
            jax.ShapeDtypeStruct((3 * rank, width), BF),
        ],
        scratch_shapes=[pltpu.VMEM((rank, width), F32), pltpu.VMEM((rank, width + 128), F32)],
        compiler_params=pltpu.CompilerParams(vmem_limit_bytes=16 * MIB),
        cost_estimate=pl.CostEstimate(
            flops=5_300_000_000, bytes_accessed=MIB, transcendentals=0
        ),
    )(p_rows)


def finish_kernel(replicas, y_parts, mix, stack, moment, q_out, error_out, buf, sems):
    rank = q_out.shape[0]
    y = y_parts[0].astype(F32)
    for k in range(1, y_parts.shape[0]):
        y = y + y_parts[k].astype(F32)
    y_hi, y_lo = split(y * (1.0 / replicas))
    a_hi, a_lo = split(mix[:, :rank])
    q_new = mm(a_hi, y_hi, NN) + mm(a_lo, y_hi, NN) + mm(a_hi, y_lo, NN)
    q_out[...] = q_new
    q_hi, q_lo = split(q_new)
    q_stack = jnp.concatenate([q_hi, q_hi, q_lo], axis=0)
    step = moment.shape[0] // CHUNKS
    puts = []
    for c in range(CHUNKS):
        cut = slice(c * step, (c + 1) * step)
        averaged = mm(stack[:, cut], q_stack, TN)
        buf[cut, :] = (moment[cut, :] - averaged).astype(BF)
        put = pltpu.make_async_copy(
            buf.at[pl.ds(c * step, step)], error_out.at[0, pl.ds(c * step, step)], sems.at[c]
        )
        put.start()
        puts.append(put)
    for put in puts:
        put.wait()


def finish(replicas, y_parts, mix, stack, moment):
    width, hidden = moment.shape
    rank = mix.shape[0]
    return pl.pallas_call(
        functools.partial(finish_kernel, replicas),
        out_specs=[IN_VMEM, IN_HBM],
        out_shape=[
            jax.ShapeDtypeStruct((rank, hidden), F32),
            jax.ShapeDtypeStruct((1, width, hidden), BF),
        ],
        scratch_shapes=[
            pltpu.VMEM((width, hidden), BF),
            pltpu.SemaphoreType.DMA((CHUNKS,)),
        ],
        compiler_params=pltpu.CompilerParams(vmem_limit_bytes=16 * MIB),
        cost_estimate=pl.CostEstimate(
            flops=2_500_000_000, bytes_accessed=4 * MIB, transcendentals=0
        ),
    )(y_parts, mix, stack, moment)


def film_kernel(core, dz_own, dz_peer, rows, scale_t, d_normed, d_scale, d_shift):
    _, width, tokens = dz_own.shape
    samples = scale_t.shape[1]
    wide = dz_own[core[0]].astype(F32) + dz_peer[core[0]].astype(F32)
    for k in range(samples):
        cut = slice(k * SEQ, (k + 1) * SEQ)
        d_normed[:, cut] = (wide[:, cut] * scale_t[:, k:k + 1]).astype(BF)
    sample = lax.broadcasted_iota(jnp.int32, (8, tokens), 0)
    token = lax.broadcasted_iota(jnp.int32, (8, tokens), 1)
    table = (token // SEQ == sample).astype(BF)
    hi, lo = split(wide * rows[...].astype(F32))
    d_scale[...] = (mm(table, hi, NT) + mm(table, lo, NT))[:samples]
    hi, lo = split(wide)
    d_shift[...] = (mm(table, hi, NT) + mm(table, lo, NT))[:samples]


def film_gradients(core, dz_own, dz_peer, rows, scale_t):
    _, width, tokens = dz_own.shape
    samples = scale_t.shape[1]
    return pl.pallas_call(
        film_kernel,
        in_specs=[pl.BlockSpec(memory_space=pltpu.SMEM)] + [IN_VMEM] * 4,
        out_shape=[
            jax.ShapeDtypeStruct((width, tokens), BF),
            jax.ShapeDtypeStruct((samples, width), F32),
            jax.ShapeDtypeStruct((samples, width), F32),
        ],
        compiler_params=pltpu.CompilerParams(vmem_limit_bytes=16 * MIB),
        cost_estimate=pl.CostEstimate(
            flops=1_100_000_000, bytes_accessed=MIB, transcendentals=0
        ),
    )(core, dz_own, dz_peer, rows, scale_t)


def local(normed, cotangent, weight, error, q_init, lengths, film_scale, film_shift):
    replicas = lax.axis_size(DP)
    col_width = normed.shape[1]
    rank, hidden = q_init.shape
    own = normed.T
    rows = lax.all_gather(own, TENSOR, axis=0, tiled=True)
    film = jnp.concatenate([film_scale, film_shift], axis=0)
    core = lax.axis_index("core")
    start = lax.axis_index(TENSOR) * col_width
    own_scale = lax.dynamic_slice_in_dim(film_scale, start, col_width, 1).T
    film, own_scale = lax.optimization_barrier((film, own_scale))
    p_error = error_share(error, q_init)
    part, z, d_pre, p_local = backward(
        lengths, rows, weight.T, weight, cotangent.T, film, p_error, q_init
    )
    moment = moment_of(z, d_pre, error)

    dz_pair = lax.psum_scatter(part, "z", scatter_dimension=0, tiled=True)
    dz_pair = dz_pair.reshape(2, col_width, -1)
    p_parts = lax.all_to_all(p_local, DP, 0, 0, tiled=True)
    p_row = jnp.sum(p_parts.astype(F32), axis=0).astype(BF)
    p_rows = lax.all_to_all(
        jnp.broadcast_to(p_row[None], (replicas,) + p_row.shape), DP, 0, 0, tiled=True
    )
    y = right_factor(p_rows, moment)
    nx, ny = lax.axis_size("x"), lax.axis_size("y")
    y_x = lax.all_to_all(jnp.broadcast_to(y[None], (nx, rank, hidden)), "x", 0, 0, tiled=True)
    y = jnp.sum(y_x.astype(F32), axis=0).astype(BF)
    p_late, _ = lax.optimization_barrier((p_rows, y))
    basis, mix, stack = gram_schmidt(p_late)
    dz_pair, _ = lax.optimization_barrier((dz_pair, mix))
    dz_peer = lax.ppermute(dz_pair, "core", SWAP)
    d_normed, d_scale, d_shift = film_gradients(
        core.reshape(1), dz_pair, dz_peer, own, own_scale
    )
    y_y = lax.all_to_all(jnp.broadcast_to(y[None], (ny, rank, hidden)), "y", 0, 0, tiled=True)
    q_new, new_error = finish(replicas, y_y, mix, stack, moment)
    return (d_normed.T, d_scale, d_shift, basis[None], q_new, new_error)


def solution(mesh):
    x, y, z = 4, 8, 8
    grid = Mesh(mesh.devices.reshape(x, y, z, 2), ("x", "y", "z", "core"))
    return jax.shard_map(
        local,
        mesh=grid,
        in_specs=(
            P(DP, TENSOR),
            P(DP, TENSOR),
            P(None, TENSOR),
            P(DP, None, TENSOR),
            P(None, TENSOR),
            P(DP),
            P(DP, None),
            P(DP, None),
        ),
        out_specs=(
            P(DP, TENSOR),
            P(DP, TENSOR),
            P(DP, TENSOR),
            P(TENSOR, None, None),
            P(None, TENSOR),
            P(DP, None, TENSOR),
        ),
        check_vma=False,
    )
```

```python
import functools

import jax
import jax.numpy as jnp
from jax import lax
from jax.experimental import pallas as pl
from jax.experimental.pallas import tpu as pltpu
from jax.sharding import Mesh, PartitionSpec as P

SEQ = 256
DP = ("x", "y")
TENSOR = ("z", "core")
SWAP = [(0, 1), (1, 0)]
BF = jnp.bfloat16
F32 = jnp.float32
NN = (((1,), (0,)), ((), ()))
NT = (((1,), (1,)), ((), ()))
TN = (((0,), (0,)), ((), ()))
MIB = 1024 * 1024
CHUNKS = 3
HALVES = 2
IN_VMEM = pl.BlockSpec(memory_space=pltpu.VMEM)
IN_HBM = pl.BlockSpec(memory_space=pltpu.HBM)


def mm(a, b, dims):
    return lax.dot_general(a, b, dims, preferred_element_type=F32)


def split(v):
    hi = v.astype(BF)
    return hi, (v - hi.astype(F32)).astype(BF)


def gelu_slope(u):
    cdf = 0.5 * (1.0 + lax.erf(u * 0.7071067811865476))
    dens = jnp.exp(-0.5 * u * u) * 0.3989422804014327
    return cdf + u * dens


def backward_kernel(lengths, rows, w_t, weight, cot_t, film, p_error, q_init,
                    part, z_out, d_out, p_out,
                    row_buf, wt_buf, w_buf, cot_buf, z_buf, part_buf, sems):
    width = rows.shape[0]
    rank = q_init.shape[0]
    samples = lengths.shape[0]
    step = width // CHUNKS
    cuts = [pl.ds(c * step, step) for c in range(CHUNKS)]
    sem = iter(range(sems.shape[0]))

    def fetch(source, target):
        copy = pltpu.make_async_copy(source, target, sems.at[next(sem)])
        copy.start()
        return copy

    get_rows = [fetch(rows.at[cuts[0]], row_buf.at[cuts[0]])]
    get_wt = fetch(w_t, wt_buf)
    get_rows += [fetch(rows.at[cut], row_buf.at[cut]) for cut in cuts[1:]]
    get_cot = fetch(cot_t, cot_buf)
    get_w = fetch(weight, w_buf)

    film_t = film[...].T
    puts = []
    for c in range(CHUNKS):
        cut = slice(c * step, (c + 1) * step)
        get_rows[c].wait()
        for k in range(samples):
            z_buf[cut, k * SEQ:(k + 1) * SEQ] = (
                row_buf[cut, k * SEQ:(k + 1) * SEQ].astype(F32) * film_t[cut, k:k + 1]
                + film_t[cut, samples + k:samples + k + 1]
            ).astype(BF)
        puts.append(fetch(z_buf.at[cuts[c]], z_out.at[cuts[c]]))
    get_wt.wait()
    get_cot.wait()
    position = lax.broadcasted_iota(jnp.int32, (1, SEQ), 1)
    halves = []
    for h in range(HALVES):
        span = samples // HALVES
        cols = slice(h * span * SEQ, (h + 1) * span * SEQ)
        u = mm(wt_buf[...], z_buf[:, cols], NN)
        valid = jnp.concatenate(
            [(position < lengths[k]).astype(F32) for k in range(h * span, (h + 1) * span)], axis=1
        )
        halves.append((cot_buf[:, cols].astype(F32) * gelu_slope(u) * valid).astype(BF))
    d_pre = jnp.concatenate(halves, axis=1)
    d_out[...] = d_pre
    get_w.wait()
    for c in range(CHUNKS):
        cut = slice(c * step, (c + 1) * step)
        part_buf[cut, :] = mm(w_buf[cut, :], d_pre, NN).astype(BF)
        puts.append(fetch(part_buf.at[cuts[c]], part.at[cuts[c]]))
    q_hi, q_lo = split(q_init[...])
    qd = mm(jnp.concatenate([q_hi, q_lo], axis=0), d_pre, NN)
    s_hi, s_lo = split(qd[:rank] + qd[rank:])
    both = mm(jnp.concatenate([s_hi, s_lo], axis=0), z_buf[...], NT)
    p = both[:rank] + both[rank:] + p_error[...]
    half = width // 2
    for k in range(rank):
        p_out[k] = jnp.concatenate([p[k:k + 1, :half], p[k:k + 1, half:]], axis=0).astype(BF)
    for put in puts:
        put.wait()


def backward(lengths, rows, w_t, weight, cot_t, film, p_error, q_init):
    width, tokens = rows.shape
    rank, hidden = q_init.shape
    return pl.pallas_call(
        backward_kernel,
        in_specs=[pl.BlockSpec(memory_space=pltpu.SMEM)]
        + [IN_HBM] * 4 + [IN_VMEM] * 3,
        out_specs=[IN_HBM, IN_HBM, IN_VMEM, IN_VMEM],
        out_shape=[
            jax.ShapeDtypeStruct((width, tokens), BF),
            jax.ShapeDtypeStruct((width, tokens), BF),
            jax.ShapeDtypeStruct((hidden, tokens), BF),
            jax.ShapeDtypeStruct((rank, 2, width // 2), BF),
        ],
        scratch_shapes=[
            pltpu.VMEM((width, tokens), BF),
            pltpu.VMEM((hidden, width), BF),
            pltpu.VMEM((width, hidden), BF),
            pltpu.VMEM((hidden, tokens), BF),
            pltpu.VMEM((width, tokens), BF),
            pltpu.VMEM((width, tokens), BF),
            pltpu.SemaphoreType.DMA((3 * CHUNKS + 3,)),
        ],
        compiler_params=pltpu.CompilerParams(vmem_limit_bytes=50 * MIB),
        cost_estimate=pl.CostEstimate(
            flops=10_000_000_000, bytes_accessed=14 * MIB, transcendentals=0
        ),
    )(lengths, rows, w_t, weight, cot_t, film, p_error, q_init)


def error_kernel(error, q_init, out):
    rank = q_init.shape[0]
    q_hi, q_lo = split(q_init[...])
    both = mm(jnp.concatenate([q_hi, q_lo], axis=0), error[0], NT)
    out[...] = both[:rank] + both[rank:]


def error_share(error, q_init):
    rank, hidden = q_init.shape
    width = error.shape[1]
    return pl.pallas_call(
        error_kernel,
        out_shape=jax.ShapeDtypeStruct((rank, width), F32),
        compiler_params=pltpu.CompilerParams(vmem_limit_bytes=16 * MIB),
        cost_estimate=pl.CostEstimate(
            flops=1_000_000_000, bytes_accessed=2 * MIB, transcendentals=0
        ),
    )(error, q_init)


def moment_kernel(z, d_pre, error, out):
    out[...] = mm(z[...], d_pre[...], NT) + error[0].astype(F32)


def moment_of(z, d_pre, error):
    width, tokens = z.shape
    hidden = d_pre.shape[0]
    step = width // CHUNKS
    return pl.pallas_call(
        moment_kernel,
        grid=(CHUNKS,),
        in_specs=[
            pl.BlockSpec((step, tokens), lambda i: (i, 0)),
            IN_VMEM,
            pl.BlockSpec((1, step, hidden), lambda i: (0, i, 0)),
        ],
        out_specs=pl.BlockSpec((step, hidden), lambda i: (i, 0)),
        out_shape=jax.ShapeDtypeStruct((width, hidden), F32),
        compiler_params=pltpu.CompilerParams(vmem_limit_bytes=20 * MIB),
        cost_estimate=pl.CostEstimate(
            flops=3_500_000_000, bytes_accessed=6 * MIB, transcendentals=0
        ),
    )(z, d_pre, error)


def right_kernel(p_rows, moment, y_out):
    rank = p_rows.shape[0]
    rows = [p_rows[k].astype(F32) for k in range(rank)]
    p = jnp.concatenate(
        [jnp.concatenate([row[h:h + 1] for row in rows], axis=0) for h in range(2)], axis=1
    ).astype(BF)
    m_hi, m_lo = split(moment[...])
    y = (mm(p, m_hi, NN) + mm(p, m_lo, NN)).astype(BF)
    for k in range(y_out.shape[0]):
        y_out[k] = y


def right_factor(p_rows, moment, copies):
    rank = p_rows.shape[0]
    width, hidden = moment.shape
    return pl.pallas_call(
        right_kernel,
        out_shape=jax.ShapeDtypeStruct((copies, rank, hidden), BF),
        compiler_params=pltpu.CompilerParams(vmem_limit_bytes=32 * MIB),
        cost_estimate=pl.CostEstimate(
            flops=600_000_000, bytes_accessed=MIB, transcendentals=0
        ),
    )(p_rows, moment)


def spread_kernel(parts, out):
    total = parts[0].astype(F32)
    for k in range(1, parts.shape[0]):
        total = total + parts[k].astype(F32)
    total = total.astype(BF)
    for k in range(out.shape[0]):
        out[k] = total


def spread(parts, copies):
    return pl.pallas_call(
        spread_kernel,
        out_shape=jax.ShapeDtypeStruct((copies,) + parts.shape[1:], BF),
        compiler_params=pltpu.CompilerParams(vmem_limit_bytes=16 * MIB),
        cost_estimate=pl.CostEstimate(
            flops=400_000_000, bytes_accessed=MIB, transcendentals=0
        ),
    )(parts)


def gram_schmidt_kernel(p_rows, basis_out, mix_out, stack_out, p, work):
    rank, _, half = p_rows.shape
    width = 2 * half
    for k in range(rank):
        row = p_rows[k].astype(F32)
        row = jnp.concatenate([row[:1], row[1:]], axis=1)
        p[k:k + 1, :] = row
        work[k:k + 1, :width] = row
    eye_row = lax.broadcasted_iota(jnp.int32, (rank, 128), 0)
    eye_col = lax.broadcasted_iota(jnp.int32, (rank, 128), 1)
    work[:, width:] = (eye_row == eye_col).astype(F32)
    for i in range(rank):
        top = i // 8 * 8
        row_id = lax.broadcasted_iota(jnp.int32, (rank - top, 1), 0) + top
        row = work[i:i + 1, :]
        main = row[:, :width]
        square = jnp.sum(main * main, axis=1, keepdims=True)
        dots = jnp.sum(p[top:, :] * main, axis=1, keepdims=True)
        inverse = 1.0 / (jnp.sqrt(square) + 1e-06)
        unit = row * inverse
        coeffs = jnp.where(row_id > i, dots * inverse, 0.0)
        work[top:, :] = jnp.where(row_id == i, unit, work[top:, :] - coeffs * unit)
    basis = work[:, :width]
    basis_out[...] = basis
    mix_out[...] = work[:, width:]
    hi, lo = split(basis)
    stack_out[...] = jnp.concatenate([hi, lo, hi], axis=0)


def gram_schmidt(p_rows):
    rank, _, half = p_rows.shape
    width = 2 * half
    return pl.pallas_call(
        gram_schmidt_kernel,
        out_shape=[
            jax.ShapeDtypeStruct((rank, width), F32),
            jax.ShapeDtypeStruct((rank, 128), F32),
            jax.ShapeDtypeStruct((3 * rank, width), BF),
        ],
        scratch_shapes=[pltpu.VMEM((rank, width), F32), pltpu.VMEM((rank, width + 128), F32)],
        compiler_params=pltpu.CompilerParams(vmem_limit_bytes=16 * MIB),
        cost_estimate=pl.CostEstimate(
            flops=5_300_000_000, bytes_accessed=MIB, transcendentals=0
        ),
    )(p_rows)


def finish_kernel(replicas, y_parts, mix, stack, moment, q_out, error_out, buf, sems):
    rank = q_out.shape[0]
    y = y_parts[0].astype(F32)
    for k in range(1, y_parts.shape[0]):
        y = y + y_parts[k].astype(F32)
    y_hi, y_lo = split(y * (1.0 / replicas))
    a_hi, a_lo = split(mix[:, :rank])
    q_new = mm(a_hi, y_hi, NN) + mm(a_lo, y_hi, NN) + mm(a_hi, y_lo, NN)
    q_out[...] = q_new
    q_hi, q_lo = split(q_new)
    q_stack = jnp.concatenate([q_hi, q_hi, q_lo], axis=0)
    step = moment.shape[0] // CHUNKS
    puts = []
    for c in range(CHUNKS):
        cut = slice(c * step, (c + 1) * step)
        averaged = mm(stack[:, cut], q_stack, TN)
        buf[cut, :] = (moment[cut, :] - averaged).astype(BF)
        put = pltpu.make_async_copy(
            buf.at[pl.ds(c * step, step)], error_out.at[0, pl.ds(c * step, step)], sems.at[c]
        )
        put.start()
        puts.append(put)
    for put in puts:
        put.wait()


def finish(replicas, y_parts, mix, stack, moment):
    width, hidden = moment.shape
    rank = mix.shape[0]
    return pl.pallas_call(
        functools.partial(finish_kernel, replicas),
        out_specs=[IN_VMEM, IN_HBM],
        out_shape=[
            jax.ShapeDtypeStruct((rank, hidden), F32),
            jax.ShapeDtypeStruct((1, width, hidden), BF),
        ],
        scratch_shapes=[
            pltpu.VMEM((width, hidden), BF),
            pltpu.SemaphoreType.DMA((CHUNKS,)),
        ],
        compiler_params=pltpu.CompilerParams(vmem_limit_bytes=16 * MIB),
        cost_estimate=pl.CostEstimate(
            flops=2_500_000_000, bytes_accessed=4 * MIB, transcendentals=0
        ),
    )(y_parts, mix, stack, moment)


def film_kernel(core, dz_own, dz_peer, rows, scale_t, d_normed, d_scale, d_shift):
    _, width, tokens = dz_own.shape
    samples = scale_t.shape[1]
    wide = dz_own[core[0]].astype(F32) + dz_peer[core[0]].astype(F32)
    for k in range(samples):
        cut = slice(k * SEQ, (k + 1) * SEQ)
        d_normed[:, cut] = (wide[:, cut] * scale_t[:, k:k + 1]).astype(BF)
    sample = lax.broadcasted_iota(jnp.int32, (8, tokens), 0)
    token = lax.broadcasted_iota(jnp.int32, (8, tokens), 1)
    table = (token // SEQ == sample).astype(BF)
    hi, lo = split(wide * rows[...].astype(F32))
    d_scale[...] = (mm(table, hi, NT) + mm(table, lo, NT))[:samples]
    hi, lo = split(wide)
    d_shift[...] = (mm(table, hi, NT) + mm(table, lo, NT))[:samples]


def film_gradients(core, dz_own, dz_peer, rows, scale_t):
    _, width, tokens = dz_own.shape
    samples = scale_t.shape[1]
    return pl.pallas_call(
        film_kernel,
        in_specs=[pl.BlockSpec(memory_space=pltpu.SMEM)] + [IN_VMEM] * 4,
        out_shape=[
            jax.ShapeDtypeStruct((width, tokens), BF),
            jax.ShapeDtypeStruct((samples, width), F32),
            jax.ShapeDtypeStruct((samples, width), F32),
        ],
        compiler_params=pltpu.CompilerParams(vmem_limit_bytes=16 * MIB),
        cost_estimate=pl.CostEstimate(
            flops=1_100_000_000, bytes_accessed=MIB, transcendentals=0
        ),
    )(core, dz_own, dz_peer, rows, scale_t)


def local(normed, cotangent, weight, error, q_init, lengths, film_scale, film_shift):
    replicas = lax.axis_size(DP)
    col_width = normed.shape[1]
    rank, hidden = q_init.shape
    own = normed.T
    rows = lax.all_gather(own, TENSOR, axis=0, tiled=True)
    film = jnp.concatenate([film_scale, film_shift], axis=0)
    core = lax.axis_index("core")
    start = lax.axis_index(TENSOR) * col_width
    own_scale = lax.dynamic_slice_in_dim(film_scale, start, col_width, 1).T
    film, own_scale = lax.optimization_barrier((film, own_scale))
    p_error = error_share(error, q_init)
    part, z, d_pre, p_local = backward(
        lengths, rows, weight.T, weight, cotangent.T, film, p_error, q_init
    )
    moment = moment_of(z, d_pre, error)

    dz_pair = lax.psum_scatter(part, "z", scatter_dimension=0, tiled=True)
    dz_pair = dz_pair.reshape(2, col_width, -1)
    p_parts = lax.all_to_all(p_local, DP, 0, 0, tiled=True)
    p_rows = lax.all_to_all(spread(p_parts, replicas), DP, 0, 0, tiled=True)
    nx, ny = lax.axis_size("x"), lax.axis_size("y")
    y_x = lax.all_to_all(right_factor(p_rows, moment, nx), "x", 0, 0, tiled=True)
    y = spread(y_x, ny)
    p_late, _ = lax.optimization_barrier((p_rows, y))
    basis, mix, stack = gram_schmidt(p_late)
    dz_pair, _ = lax.optimization_barrier((dz_pair, mix))
    dz_peer = lax.ppermute(dz_pair, "core", SWAP)
    d_normed, d_scale, d_shift = film_gradients(
        core.reshape(1), dz_pair, dz_peer, own, own_scale
    )
    y_y = lax.all_to_all(y, "y", 0, 0, tiled=True)
    q_new, new_error = finish(replicas, y_y, mix, stack, moment)
    return (d_normed.T, d_scale, d_shift, basis[None], q_new, new_error)


def solution(mesh):
    x, y, z = 4, 8, 8
    grid = Mesh(mesh.devices.reshape(x, y, z, 2), ("x", "y", "z", "core"))
    return jax.shard_map(
        local,
        mesh=grid,
        in_specs=(
            P(DP, TENSOR),
            P(DP, TENSOR),
            P(None, TENSOR),
            P(DP, None, TENSOR),
            P(None, TENSOR),
            P(DP),
            P(DP, None),
            P(DP, None),
        ),
        out_specs=(
            P(DP, TENSOR),
            P(DP, TENSOR),
            P(DP, TENSOR),
            P(TENSOR, None, None),
            P(None, TENSOR),
            P(DP, None, TENSOR),
        ),
        check_vma=False,
    )
```
